512 devices in a mesh: blk: 64 (over y, z_lo, core), hid: 8 (over x, z_hi).
Axes of the slice: x: 4, y: 4, z: 16 (z_hi: 2, z_lo: 8; z = z_hi * 8 + z_lo), core: 2. Of those that a mesh axis runs over, the one named last changes fastest.
Arguments:
- features: bfloat16 [8192, 128], P('blk'), may hold values from -6 to 6
- tile_values: bfloat16 [64, 8, 32, 128, 128], P('blk', 'hid'), may hold values from -0.03125 to 0.03125
- tile_block: int32 [64, 8, 32], P('blk', 'hid'), may hold values from 0 to 63, as said below
- weight: bfloat16 [128, 256], P(None, 'hid'), may hold values from -0.5 to 0.5
- bias: float32 [256], P('hid'), may hold values from -3 to 3
- cotangent: bfloat16 [8192, 256], P('blk', 'hid'), may hold values from -6 to 6
Outputs:
- activations: bfloat16 [8192, 256], P('blk', 'hid')
- feature_grad: float32 [8192, 128], P('blk')
- weight_grad: float32 [128, 256], P(None, 'hid')
- bias_grad: float32 [256], P('hid')
The draws below stay inside these ranges and needn't reach their ends.
Inputs may be any that keep to these rules, and one draw needn't show every extreme that they name: `tile_block`: each device's list (fixed i, j) is sorted by source block and names each block at most 3 times; it names its own row block i exactly 3 times and at least one other block exactly 3 times.
All inputs are finite; a program needn't handle non-finite values.
Results may differ from the reference program's by a relative error of at most 0.017.
Values may be sent and summed in bfloat16 or wider, within the bound.
No kernel may reach another device: no remote copies, remote signals or barrier semaphores. Data moves between devices by JAX's collectives and lax.ppermute only.
A program may use at most 64 MiB of HBM per device.

```python
import jax
import jax.numpy as jnp
from jax import lax

F = 128
H = 256
TILE = 128
KSTEP = 3
TILES_DEV = 32
NODES = 8192
N_BLK = 64
N_HID = 8


def draw_tile_block(key, part):
    key = jax.random.fold_in(key, 11)
    key_other, key_order = jax.random.split(key)
    slot_count = (N_BLK - 2) * KSTEP
    spare_count = TILES_DEV - 2 * KSTEP
    own_block = jnp.arange(N_BLK, dtype=jnp.int32)[:, None, None]
    second = jax.random.randint(key_other, (N_BLK, N_HID, 1), 1, N_BLK).astype(jnp.int32)
    scores = jax.random.randint(key_order, (N_BLK, N_HID, slot_count), 0, 1 << 20).astype(jnp.int32) * slot_count + jnp.arange(slot_count, dtype=jnp.int32)
    ranked = jnp.argsort(scores, axis=-1)[..., :spare_count].astype(jnp.int32)
    offset = 1 + ranked // KSTEP
    offset = offset + (offset >= second).astype(jnp.int32)
    picked = jnp.concatenate([jnp.zeros((N_BLK, N_HID, KSTEP), jnp.int32), jnp.broadcast_to(second, (N_BLK, N_HID, KSTEP)), offset], axis=-1)
    return jnp.sort((own_block + picked) % N_BLK, axis=-1).astype(jnp.int32)


def level_of(rng, extent, cuts, smallest, high):
    def one(dim, blocks):
        draws = jax.random.uniform(jax.random.fold_in(jax.random.fold_in(rng, 6), dim), (blocks,), jnp.float32, smallest / len(cuts), high / len(cuts))
        return jnp.repeat(jnp.exp(draws), extent[dim] // blocks).reshape((-1,) + (1,) * (len(extent) - dim - 1))

    factor_of = one(*cuts[0])
    for cut in cuts[1:]:
        factor_of = factor_of * one(*cut)
    return factor_of


def normal_values(stream_key, dims, deviation, most, pieces=(), held_as=jnp.bfloat16):
    array = deviation * jax.random.normal(stream_key, dims, jnp.float32)
    if pieces:
        array = array * level_of(stream_key, dims, pieces, -0.22, 0.18)
    return jnp.clip(array, -most, most).astype(held_as)


def setup_inputs(seed: int = 0) -> dict:
    key_of = jax.random.split(jax.random.key(seed), 7)
    features = normal_values(key_of[0], (NODES, F), 1.0, 6.0, ((0, 64),))
    tile_values = normal_values(key_of[1], (N_BLK, N_HID, TILES_DEV, TILE, TILE), (N_HID * TILES_DEV * TILE) ** -0.5, 0.03125, ((0, 64), (1, 8)))
    tile_block = draw_tile_block(jax.random.fold_in(key_of[6], 71), 0)
    weight = normal_values(key_of[3], (F, H), F ** -0.5, 0.5, ((1, 8),))
    bias = normal_values(key_of[4], (H,), 0.5, 3.0, ((0, 8),), jnp.float32)
    cotangent = normal_values(key_of[5], (NODES, H), 1.0, 6.0, ((0, 64), (1, 8)))
    return {"features": features, "tile_values": tile_values, "tile_block": tile_block, "weight": weight, "bias": bias, "cotangent": cotangent}


def reference(features, tile_values, tile_block, weight, bias, cotangent):
    row_blocks = features.reshape(N_BLK, TILE, F)
    all_vals = tile_values.reshape(N_BLK, N_HID * TILES_DEV, TILE, TILE)
    all_src = tile_block.reshape(N_BLK, N_HID * TILES_DEV).astype(jnp.int32)

    def aggregate_row(operands):
        tile_vals, tile_src = operands
        sources = jnp.take(row_blocks, tile_src, axis=0).astype(jnp.float32)
        return jnp.einsum('kab,kbf->af', tile_vals.astype(jnp.float32), sources)
    summed = lax.map(aggregate_row, (all_vals, all_src))
    aggregated = summed.reshape(NODES, F).astype(jnp.bfloat16)
    preact = jnp.dot(aggregated, weight, preferred_element_type=jnp.float32) + bias
    activations = jax.nn.gelu(preact).astype(jnp.bfloat16)
    _, pullback = jax.vjp(jax.nn.gelu, preact)
    pre_grad = pullback(cotangent.astype(jnp.float32))[0].astype(jnp.bfloat16)
    back_feat = jnp.dot(pre_grad, weight.T, preferred_element_type=jnp.float32).astype(jnp.bfloat16)
    back_blocks = back_feat.reshape(N_BLK, TILE, F)

    def spread_row(running, operands):
        tile_vals, tile_src, rows_back = operands
        contrib = jnp.einsum('kab,af->kbf', tile_vals.astype(jnp.float32), rows_back.astype(jnp.float32))
        return (running.at[tile_src].add(contrib), None)
    start_acc = jnp.zeros((N_BLK, TILE, F), jnp.float32)
    spread, _ = lax.scan(spread_row, start_acc, (all_vals, all_src, back_blocks))
    feature_grad = spread.reshape(NODES, F)
    weight_grad = lax.dot_general(aggregated, pre_grad, (((0,), (0,)), ((), ())), preferred_element_type=jnp.float32)
    bias_grad = lax.optimization_barrier(jnp.sum(pre_grad.astype(jnp.float32), axis=0))
    return (activations, feature_grad, weight_grad, bias_grad)
```

```python
import functools

import jax
import jax.numpy as jnp
from jax import lax
from jax.experimental import pallas as pl
from jax.experimental.pallas import tpu as pltpu
from jax.sharding import Mesh
from jax.sharding import PartitionSpec as P

BF16 = jnp.bfloat16
F32 = jnp.float32
AXES = ("y", "zl", "c", "x", "zh")
BLK = ("y", "zl", "c")
HID = ("x", "zh")
EXTRA = 16
SCALE = 0.7978845608028654
CUBIC = 0.044715
PARAMS = pltpu.CompilerParams(vmem_limit_bytes=48 * 1024 * 1024)


def mm(a, b, ca, cb):
    return lax.dot_general(a, b, (((ca,), (cb,)), ((), ())), preferred_element_type=F32)


def slope(v):
    t = jnp.tanh(SCALE * (v + CUBIC * (v * v * v)))
    du = SCALE * (1.0 + (3.0 * CUBIC) * (v * v))
    return 0.5 * (1.0 + t) + 0.5 * v * (1.0 - t * t) * du


def place(src, zl_n):
    return src // (2 * zl_n), (src // 2) % zl_n, src % 2


def forward_kernel(zl_n, x_n, src_ref, tiles_ref, own_ref, oth_ref, out_ref):
    my_c = lax.axis_index("c")
    tile = tiles_ref.shape[-1]
    feat = own_ref.shape[-1]
    acc = jnp.zeros((tile, feat), F32)
    n = tiles_ref.shape[0]
    for k in range(0, n, 2):
        blocks = []
        for q in range(k, k + 2):
            y, zl, c = place(src_ref[q], zl_n)
            a = own_ref[pl.ds(y, 1), :, pl.ds(zl, 1)].reshape(tile, feat)
            b = oth_ref[pl.ds(y, 1), :, pl.ds(zl, 1)].reshape(tile, feat)
            blocks.append(jnp.where(c == my_c, a, b))
        lhs = jnp.concatenate([tiles_ref[k], tiles_ref[k + 1]], axis=1)
        acc = acc + mm(lhs, jnp.concatenate(blocks, axis=0), 1, 0)
    part = acc.astype(BF16)
    for x in range(x_n):
        out_ref[x] = part


def backward_kernel(
    zl_n, src_ref, sum_ref, other_ref, packs_ref, pack_ref, bias_ref, tiles_ref, act_ref, own_ref, oth_ref
):
    my_c = lax.axis_index("c")
    x_n, zh_n = packs_ref.shape[:2]
    hidden = bias_ref.shape[1]
    tile = tiles_ref.shape[-1]
    y_n = own_ref.shape[0] // x_n
    rows = tile // x_n
    agg = (sum_ref[...].astype(F32) + other_ref[...].astype(F32)).astype(BF16)

    def gather(start, size):
        parts = [packs_ref[x, z, start : start + size, :] for x in range(x_n) for z in range(zh_n)]
        return jnp.concatenate(parts, axis=0)

    def bias_of(three):
        return mm(three, jnp.ones((three.shape[0], tile), BF16), 0, 0)[:hidden]

    w_t = gather(0, hidden)
    cot_t = gather(hidden, hidden)
    bias_t = jnp.concatenate(
        [bias_of(packs_ref[x, z, 2 * hidden :, :]) for x in range(x_n) for z in range(zh_n)], axis=0
    )
    pre_t = mm(w_t, agg, 1, 1) + bias_t
    grad_t = (cot_t.astype(F32) * slope(pre_t)).astype(BF16)
    back = mm(grad_t, w_t, 0, 0).astype(BF16)

    w_mine = pack_ref[0:hidden, :]
    pre = mm(agg, w_mine, 1, 1) + bias_ref[...]
    t = jnp.tanh(SCALE * (pre + CUBIC * (pre * pre * pre)))
    act_ref[...] = (pre * (0.5 * (1.0 + t))).astype(BF16)
    mine_t = mm(w_mine, agg, 1, 1) + bias_of(pack_ref[2 * hidden :, :])
    grad_mine = (pack_ref[hidden : 2 * hidden, :].astype(F32) * slope(mine_t)).astype(BF16)
    wgrad = mm(grad_mine, agg, 1, 0).astype(BF16)
    bgrad = mm(jnp.ones((8, tile), BF16), grad_mine, 1, 1)
    bgrad = jnp.concatenate([bgrad, jnp.zeros((8, tile - hidden), F32)], axis=1).astype(BF16)

    body = zl_n * rows
    share = hidden // y_n
    assert share <= 8
    own_ref[:, :body, :] = jnp.zeros((y_n * x_n, body, tile), BF16)
    oth_ref[:, :body, :] = jnp.zeros((y_n * x_n, body, tile), BF16)
    for y in range(y_n):
        piece = [wgrad[y * share : (y + 1) * share].astype(F32), bgrad.astype(F32)]
        if share < 8:
            piece.insert(1, jnp.zeros((8 - share, tile), F32))
        piece = jnp.concatenate(piece, axis=0).astype(BF16)
        for x in range(x_n):
            own_ref[y * x_n + x, body:, :] = piece
            oth_ref[y * x_n + x, body:, :] = piece

    acc = jnp.zeros((tile, tile), F32)
    for k in range(tiles_ref.shape[0]):
        src = src_ref[k]
        contrib = mm(tiles_ref[k], back, 0, 0)
        if k:
            acc = contrib + jnp.where(src == src_ref[k - 1], acc, 0.0)
        else:
            acc = contrib
        y, zl, c = place(src, zl_n)
        out = acc.astype(BF16).reshape(x_n, rows, tile)
        at = (pl.ds(y * x_n, x_n), pl.ds(pl.multiple_of(zl * rows, rows), rows), slice(None))

        @pl.when(c == my_c)
        def _():
            own_ref[at] = out

        @pl.when(c != my_c)
        def _():
            oth_ref[at] = out


def plane_sum_kernel(y_n, x_n, in_ref, out_ref):
    my_x = lax.axis_index("x")
    zl_n, zh_n, size, _ = out_ref.shape
    rows = size - EXTRA
    body = zl_n * rows
    total = in_ref[0, :body, :].astype(F32)
    for s in range(1, y_n * x_n):
        total = total + in_ref[s, :body, :].astype(F32)
    extra = in_ref[my_x, body:, :].astype(F32)
    for y in range(1, y_n):
        extra = extra + in_ref[y * x_n + my_x, body:, :].astype(F32)
    total = total.astype(BF16)
    extra = extra.astype(BF16)
    for z in range(zl_n):
        for h in range(zh_n):
            out_ref[z, h, :rows, :] = total[z * rows : (z + 1) * rows]
            out_ref[z, h, rows:, :] = extra


def column_sum_kernel(zl_n, zh_n, in_ref, out_ref):
    my_zh = lax.axis_index("zh")
    rows = in_ref.shape[1] - EXTRA
    total = in_ref[0, :rows, :].astype(F32)
    for s in range(1, zl_n * zh_n):
        total = total + in_ref[s, :rows, :].astype(F32)
    extra = in_ref[my_zh, rows:, :].astype(F32)
    for z in range(1, zl_n):
        extra = extra + in_ref[z * zh_n + my_zh, rows:, :].astype(F32)
    for s in range(out_ref.shape[0]):
        out_ref[s, :rows, :] = total.astype(out_ref.dtype)
        out_ref[s, rows:, :] = extra.astype(out_ref.dtype)


def finish_kernel(y_n, x_n, in_ref, feat_ref, wgrad_ref, bgrad_ref):
    my_x, my_y = lax.axis_index("x"), lax.axis_index("y")
    rows = in_ref.shape[1] - EXTRA
    hidden = bgrad_ref.shape[1]
    share = hidden // y_n
    for x in range(x_n):
        feat_ref[x * rows : (x + 1) * rows, :] = in_ref[my_y * x_n + x, :rows, :].astype(F32)
    pieces = [in_ref[y * x_n + my_x, rows:, :].astype(F32) for y in range(y_n)]
    wgrad_ref[...] = jnp.concatenate([p[:share] for p in pieces], axis=0).T
    bgrad_ref[...] = pieces[0][8:9, :hidden]


VMEM = pl.BlockSpec(memory_space=pltpu.VMEM)
SMEM = pl.BlockSpec(memory_space=pltpu.SMEM)


def shape(*dims, dtype=BF16):
    return jax.ShapeDtypeStruct(dims, dtype)


def call(kernel, out, *args, smem=0):
    many = isinstance(out, (tuple, list))
    return pl.pallas_call(
        kernel,
        out_shape=out,
        in_specs=[SMEM] * smem + [VMEM] * (len(args) - smem),
        out_specs=[VMEM] * len(out) if many else VMEM,
        compiler_params=PARAMS,
    )(*args)


def to_all(v, axes):
    return lax.all_to_all(v, axes, 0, 0, tiled=True)


def swap(v, axis):
    return lax.ppermute(v, axis, [(0, 1), (1, 0)])


def on_device(sizes, features, tile_values, tile_block, weight, bias, cotangent):
    y_n, zl_n, c_n, x_n, zh_n = (sizes[a] for a in AXES)
    tile = tile_values.shape[-1]
    feat = features.shape[1]
    hidden = bias.shape[0]
    rows = tile // x_n
    tiles = tile_values.reshape(-1, tile, tile)
    sources = tile_block.reshape(-1)
    my_x, my_zh = lax.axis_index("x"), lax.axis_index("zh")

    b_hi = bias.astype(BF16)
    b_mid = (bias - b_hi.astype(F32)).astype(BF16)
    b_lo = (bias - b_hi.astype(F32) - b_mid.astype(F32)).astype(BF16)
    terms = jnp.pad(jnp.stack([b_hi, b_mid, b_lo]), ((0, 13), (0, feat - hidden)))
    pack = jnp.concatenate([weight.T, cotangent.T, terms], axis=0)
    pack_other = swap(pack, "zh")

    mine = lax.dynamic_slice_in_dim(features, my_x * rows, rows, 0)
    column = to_all(jnp.broadcast_to(mine[None], (zl_n, rows, feat)), "zl")
    pair = jnp.where(my_zh == 0, jnp.stack([pack, pack_other]), jnp.stack([pack_other, pack]))
    packs = to_all(jnp.broadcast_to(pair[None], (x_n,) + pair.shape), "x")
    plane = to_all(jnp.broadcast_to(column[None], (y_n * x_n, zl_n, rows, feat)), ("y", "x"))
    own = plane.reshape(y_n, x_n, zl_n, rows, feat)
    other = swap(own, "c")

    part = call(
        functools.partial(forward_kernel, zl_n, x_n), shape(x_n, tile, feat), sources, tiles, own, other, smem=1
    )
    summed = jnp.sum(to_all(part, "x").astype(F32), axis=0).astype(BF16)
    summed_other = swap(summed, "zh")

    payload = shape(y_n * x_n, zl_n * rows + EXTRA, feat)
    activations, keep, give = call(
        functools.partial(backward_kernel, zl_n),
        (shape(tile, hidden), payload, payload),
        sources,
        summed,
        summed_other,
        packs,
        pack,
        bias[None],
        tiles,
        smem=1,
    )
    both = (keep.astype(F32) + swap(give, "c").astype(F32)).astype(BF16)
    across = to_all(both, ("y", "x"))
    up = call(
        functools.partial(plane_sum_kernel, y_n, x_n), shape(zl_n, zh_n, rows + EXTRA, feat), across
    ).reshape(zl_n * zh_n, rows + EXTRA, feat)
    down = to_all(up, ("zl", "zh"))
    last = call(
        functools.partial(column_sum_kernel, zl_n, zh_n), shape(y_n * x_n, rows + EXTRA, feat), down
    )
    feature_grad, weight_grad, bias_grad = call(
        functools.partial(finish_kernel, y_n, x_n),
        (shape(tile, feat, dtype=F32), shape(feat, hidden, dtype=F32), shape(1, hidden, dtype=F32)),
        to_all(last, ("y", "x")),
    )
    return activations, feature_grad, weight_grad, bias_grad[0]


def split_mesh(mesh, sizes):
    return Mesh(mesh.devices.reshape(tuple(sizes[a] for a in AXES)), AXES)


def solution(mesh, sizes=None):
    sizes = sizes or {"y": 4, "zl": 8, "c": 2, "x": 4, "zh": 2}
    placed = (
        P(BLK, None),
        P(BLK, HID, None, None, None),
        P(BLK, HID, None),
        P(None, HID),
        P(HID),
        P(BLK, HID),
    )
    return jax.shard_map(
        functools.partial(on_device, sizes),
        mesh=split_mesh(mesh, sizes),
        in_specs=placed,
        out_specs=(P(BLK, HID), P(BLK, None), P(None, HID), P(HID)),
        check_vma=False,
    )
```

```python
import functools

import jax
import jax.numpy as jnp
from jax import lax
from jax.experimental import pallas as pl
from jax.experimental.pallas import tpu as pltpu
from jax.sharding import Mesh
from jax.sharding import PartitionSpec as P

BF16 = jnp.bfloat16
F32 = jnp.float32
AXES = ("y", "zl", "c", "x", "zh")
BLK = ("y", "zl", "c")
HID = ("x", "zh")
EXTRA = 16
SCALE = 0.7978845608028654
CUBIC = 0.044715
PARAMS = pltpu.CompilerParams(vmem_limit_bytes=48 * 1024 * 1024)


def mm(a, b, ca, cb):
    return lax.dot_general(a, b, (((ca,), (cb,)), ((), ())), preferred_element_type=F32)


def slope(v):
    t = jnp.tanh(SCALE * (v + CUBIC * (v * v * v)))
    du = SCALE * (1.0 + (3.0 * CUBIC) * (v * v))
    return 0.5 * (1.0 + t) + 0.5 * v * (1.0 - t * t) * du


def place(src, zl_n):
    return src // (2 * zl_n), (src // 2) % zl_n, src % 2


def forward_kernel(zl_n, x_n, src_ref, tiles_ref, own_ref, oth_ref, pack_ref, pack_other_ref, out_ref):
    my_c = lax.axis_index("c")
    tile = tiles_ref.shape[-1]
    feat = own_ref.shape[-1]
    size = pack_ref.shape[0]
    acc = jnp.zeros((tile, feat), F32)
    n = tiles_ref.shape[0]
    for k in range(0, n, 2):
        blocks = []
        for q in range(k, k + 2):
            y, zl, c = place(src_ref[q], zl_n)
            a = own_ref[pl.ds(y, 1), :, pl.ds(zl, 1)].reshape(tile, feat)
            b = oth_ref[pl.ds(y, 1), :, pl.ds(zl, 1)].reshape(tile, feat)
            blocks.append(jnp.where(c == my_c, a, b))
        lhs = jnp.concatenate([tiles_ref[k], tiles_ref[k + 1]], axis=1)
        acc = acc + mm(lhs, jnp.concatenate(blocks, axis=0), 1, 0)
    part = acc.astype(BF16)
    for x in range(x_n):
        out_ref[x, :tile, :] = part
        out_ref[x, tile : tile + size, :] = pack_ref[...]
        out_ref[x, tile + size :, :] = pack_other_ref[...]


def backward_kernel(zl_n, src_ref, sum_ref, other_ref, packs_ref, pack_ref, tiles_ref, act_ref, out_ref):
    my_c = lax.axis_index("c")
    x_n = packs_ref.shape[0]
    hidden = act_ref.shape[0]
    tile = tiles_ref.shape[-1]
    size = pack_ref.shape[0]
    y_n = out_ref.shape[1] // x_n
    rows = tile // x_n
    agg = (sum_ref[...].astype(F32) + other_ref[...].astype(F32)).astype(BF16)
    starts = [(x, tile + z * size) for x in range(x_n) for z in range(2)]

    def gather(start, count):
        return jnp.concatenate([packs_ref[x, at + start : at + start + count, :] for x, at in starts], axis=0)

    def bias_of(three):
        return mm(three, jnp.ones((three.shape[0], tile), BF16), 0, 0)[:hidden]

    w_t = gather(0, hidden)
    cot_t = gather(hidden, hidden)
    bias_t = jnp.concatenate([bias_of(packs_ref[x, at + 2 * hidden : at + size, :]) for x, at in starts], axis=0)
    pre_t = mm(w_t, agg, 1, 1) + bias_t
    grad_t = (cot_t.astype(F32) * slope(pre_t)).astype(BF16)
    back_t = mm(w_t, grad_t, 0, 0).astype(BF16)

    w_mine = pack_ref[0:hidden, :]
    mine_t = mm(w_mine, agg, 1, 1) + bias_of(pack_ref[2 * hidden :, :])
    t = jnp.tanh(SCALE * (mine_t + CUBIC * (mine_t * mine_t * mine_t)))
    act_ref[...] = (mine_t * (0.5 * (1.0 + t))).astype(BF16)
    grad_mine = (pack_ref[hidden : 2 * hidden, :].astype(F32) * slope(mine_t)).astype(BF16)
    wgrad = mm(grad_mine, agg, 1, 0)
    bgrad = mm(jnp.ones((8, tile), BF16), grad_mine, 1, 1)
    bgrad = jnp.concatenate([bgrad, jnp.zeros((8, tile - hidden), F32)], axis=1)

    body = zl_n * rows
    share = hidden // y_n
    assert share <= 8
    out_ref[:, :, :body, :] = jnp.zeros((2, y_n * x_n, body, tile), BF16)
    for y in range(y_n):
        piece = [wgrad[y * share : (y + 1) * share], bgrad]
        if share < 8:
            piece.insert(1, jnp.zeros((8 - share, tile), F32))
        piece = jnp.concatenate(piece, axis=0).astype(BF16)
        for x in range(x_n):
            out_ref[0, y * x_n + x, body:, :] = piece
            out_ref[1, y * x_n + x, body:, :] = piece

    acc = None
    for k in range(0, tiles_ref.shape[0], 2):
        pair = mm(back_t, jnp.concatenate([tiles_ref[k], tiles_ref[k + 1]], axis=1), 1, 0)
        for q, contrib in ((k, pair[:, :tile]), (k + 1, pair[:, tile:])):
            src = src_ref[q]
            if q:
                contrib = contrib + jnp.where(src == src_ref[q - 1], acc, 0.0)
            acc = contrib
            y, zl, c = place(src, zl_n)
            away = jnp.where(c == my_c, 0, 1)
            at = (pl.ds(away, 1), pl.ds(y * x_n, x_n), pl.ds(pl.multiple_of(zl * rows, rows), rows), slice(None))
            out_ref[at] = acc.astype(BF16).reshape(1, x_n, rows, tile)


def plane_sum_kernel(y_n, x_n, in_ref, out_ref):
    my_x = lax.axis_index("x")
    zl_n, zh_n, size, _ = out_ref.shape
    rows = size - EXTRA
    body = zl_n * rows
    total = in_ref[0, :body, :].astype(F32)
    for s in range(1, y_n * x_n):
        total = total + in_ref[s, :body, :].astype(F32)
    extra = in_ref[my_x, body:, :].astype(F32)
    for y in range(1, y_n):
        extra = extra + in_ref[y * x_n + my_x, body:, :].astype(F32)
    total = total.astype(BF16)
    extra = extra.astype(BF16)
    for z in range(zl_n):
        for h in range(zh_n):
            out_ref[z, h, :rows, :] = total[z * rows : (z + 1) * rows]
            out_ref[z, h, rows:, :] = extra


def column_sum_kernel(zl_n, zh_n, in_ref, out_ref):
    my_zh = lax.axis_index("zh")
    rows = in_ref.shape[1] - EXTRA
    total = in_ref[0, :rows, :].astype(F32)
    for s in range(1, zl_n * zh_n):
        total = total + in_ref[s, :rows, :].astype(F32)
    extra = in_ref[my_zh, rows:, :].astype(F32)
    for z in range(1, zl_n):
        extra = extra + in_ref[z * zh_n + my_zh, rows:, :].astype(F32)
    for s in range(out_ref.shape[0]):
        out_ref[s, :rows, :] = total.astype(out_ref.dtype)
        out_ref[s, rows:, :] = extra.astype(out_ref.dtype)


def finish_kernel(y_n, x_n, in_ref, feat_ref, wgrad_ref, bgrad_ref):
    my_x, my_y = lax.axis_index("x"), lax.axis_index("y")
    rows = in_ref.shape[1] - EXTRA
    hidden = bgrad_ref.shape[1]
    share = hidden // y_n
    feat_ref[...] = jnp.concatenate(
        [in_ref[my_y * x_n + x, :rows, :].astype(F32) for x in range(x_n)], axis=0
    ).T
    pieces = [in_ref[y * x_n + my_x, rows:, :].astype(F32) for y in range(y_n)]
    wgrad_ref[...] = jnp.concatenate([p[:share] for p in pieces], axis=0)
    bgrad_ref[...] = pieces[0][8:9, :hidden]


VMEM = pl.BlockSpec(memory_space=pltpu.VMEM)
SMEM = pl.BlockSpec(memory_space=pltpu.SMEM)


def shape(*dims, dtype=BF16):
    return jax.ShapeDtypeStruct(dims, dtype)


def call(kernel, out, *args, smem=0):
    many = isinstance(out, (tuple, list))
    return pl.pallas_call(
        kernel,
        out_shape=out,
        in_specs=[SMEM] * smem + [VMEM] * (len(args) - smem),
        out_specs=[VMEM] * len(out) if many else VMEM,
        compiler_params=PARAMS,
    )(*args)


def to_all(v, axes):
    return lax.all_to_all(v, axes, 0, 0, tiled=True)


def swap(v, axis):
    return lax.ppermute(v, axis, [(0, 1), (1, 0)])


def on_device(sizes, features, tile_values, tile_block, weight, bias, cotangent):
    y_n, zl_n, c_n, x_n, zh_n = (sizes[a] for a in AXES)
    tile = tile_values.shape[-1]
    feat = features.shape[1]
    hidden = bias.shape[0]
    rows = tile // x_n
    tiles = tile_values.reshape(-1, tile, tile)
    sources = tile_block.reshape(-1)
    my_x = lax.axis_index("x")

    b_hi = bias.astype(BF16)
    b_mid = (bias - b_hi.astype(F32)).astype(BF16)
    b_lo = (bias - b_hi.astype(F32) - b_mid.astype(F32)).astype(BF16)
    terms = jnp.pad(jnp.stack([b_hi, b_mid, b_lo]), ((0, 13), (0, feat - hidden)))
    pack = jnp.concatenate([weight.T, cotangent.T, terms], axis=0)
    pack_other = swap(pack, "zh")

    mine = lax.dynamic_slice_in_dim(features, my_x * rows, rows, 0)
    column = to_all(jnp.broadcast_to(mine[None], (zl_n, rows, feat)), "zl")
    column, pack_other = lax.optimization_barrier((column, pack_other))
    plane = to_all(jnp.broadcast_to(column[None], (y_n * x_n, zl_n, rows, feat)), ("y", "x"))
    own = plane.reshape(y_n, x_n, zl_n, rows, feat)
    other = swap(own, "c")

    size = pack.shape[0]
    part = to_all(
        call(
            functools.partial(forward_kernel, zl_n, x_n),
            shape(x_n, tile + 2 * size, feat),
            sources,
            tiles,
            own,
            other,
            pack,
            pack_other,
            smem=1,
        ),
        "x",
    )
    summed = jnp.sum(part[:, :tile].astype(F32), axis=0).astype(BF16)
    summed_other = swap(summed, "zh")

    act_t, pieces = call(
        functools.partial(backward_kernel, zl_n),
        (shape(hidden, tile), shape(2, y_n * x_n, zl_n * rows + EXTRA, feat)),
        sources,
        summed,
        summed_other,
        part,
        pack,
        tiles,
        smem=1,
    )
    both = (pieces[0].astype(F32) + swap(pieces[1], "c").astype(F32)).astype(BF16)
    across = to_all(both, ("y", "x"))
    up = call(
        functools.partial(plane_sum_kernel, y_n, x_n), shape(zl_n, zh_n, rows + EXTRA, feat), across
    ).reshape(zl_n * zh_n, rows + EXTRA, feat)
    down = to_all(up, ("zl", "zh"))
    last = call(
        functools.partial(column_sum_kernel, zl_n, zh_n), shape(y_n * x_n, rows + EXTRA, feat), down
    )
    feature_grad, wgrad_t, bias_grad = call(
        functools.partial(finish_kernel, y_n, x_n),
        (shape(tile, feat, dtype=F32), shape(hidden, feat, dtype=F32), shape(1, hidden, dtype=F32)),
        to_all(last, ("y", "x")),
    )
    return act_t.T, feature_grad, wgrad_t.T, bias_grad[0]


def split_mesh(mesh, sizes):
    return Mesh(mesh.devices.reshape(tuple(sizes[a] for a in AXES)), AXES)


def solution(mesh, sizes=None):
    sizes = sizes or {"y": 4, "zl": 8, "c": 2, "x": 4, "zh": 2}
    placed = (
        P(BLK, None),
        P(BLK, HID, None, None, None),
        P(BLK, HID, None),
        P(None, HID),
        P(HID),
        P(BLK, HID),
    )
    return jax.shard_map(
        functools.partial(on_device, sizes),
        mesh=split_mesh(mesh, sizes),
        in_specs=placed,
        out_specs=(P(BLK, HID), P(BLK, None), P(None, HID), P(HID)),
        check_vma=False,
    )
```

```python
import functools

import jax
import jax.numpy as jnp
from jax import lax
from jax.experimental import pallas as pl
from jax.experimental.pallas import tpu as pltpu
from jax.sharding import Mesh
from jax.sharding import PartitionSpec as P

BF16 = jnp.bfloat16
F32 = jnp.float32
AXES = ("y", "zl", "c", "x", "zh")
BLK = ("y", "zl", "c")
HID = ("x", "zh")
EXTRA = 16
SCALE = 0.7978845608028654
CUBIC = 0.044715
PARAMS = pltpu.CompilerParams(vmem_limit_bytes=48 * 1024 * 1024)


def mm(a, b, ca, cb):
    return lax.dot_general(a, b, (((ca,), (cb,)), ((), ())), preferred_element_type=F32)


def slope(v):
    t = jnp.tanh(SCALE * (v + CUBIC * (v * v * v)))
    du = SCALE * (1.0 + (3.0 * CUBIC) * (v * v))
    return 0.5 * (1.0 + t) + 0.5 * v * (1.0 - t * t) * du


def place(src, zl_n):
    return src // (2 * zl_n), (src // 2) % zl_n, src % 2


def forward_kernel(zl_n, x_n, src_ref, tiles_ref, own_ref, oth_ref, pack_ref, pack_other_ref, out_ref):
    my_c = lax.axis_index("c")
    tile = tiles_ref.shape[-1]
    feat = own_ref.shape[-1]
    size = pack_ref.shape[0]
    acc = jnp.zeros((tile, feat), F32)
    n = tiles_ref.shape[0]
    for k in range(0, n, 2):
        blocks = []
        for q in range(k, k + 2):
            y, zl, c = place(src_ref[q], zl_n)
            a = own_ref[pl.ds(y, 1), :, pl.ds(zl, 1)].reshape(tile, feat)
            b = oth_ref[pl.ds(y, 1), :, pl.ds(zl, 1)].reshape(tile, feat)
            blocks.append(jnp.where(c == my_c, a, b))
        lhs = jnp.concatenate([tiles_ref[k], tiles_ref[k + 1]], axis=1)
        acc = acc + mm(lhs, jnp.concatenate(blocks, axis=0), 1, 0)
    part = acc.astype(BF16)
    for x in range(x_n):
        out_ref[x, :tile, :] = part
        out_ref[x, tile : tile + size, :] = pack_ref[...]
        out_ref[x, tile + size :, :] = pack_other_ref[...]


def backward_kernel(zl_n, src_ref, sum_ref, other_ref, packs_ref, pack_ref, tiles_ref, act_ref, out_ref):
    my_c = lax.axis_index("c")
    x_n = packs_ref.shape[0]
    hidden = act_ref.shape[0]
    tile = tiles_ref.shape[-1]
    size = pack_ref.shape[0]
    y_n = out_ref.shape[1] // x_n
    rows = tile // x_n
    agg = (sum_ref[...].astype(F32) + other_ref[...].astype(F32)).astype(BF16)
    starts = [(x, tile + z * size) for x in range(x_n) for z in range(2)]

    def gather(start, count):
        return jnp.concatenate([packs_ref[x, at + start : at + start + count, :] for x, at in starts], axis=0)

    def bias_of(three):
        return mm(three, jnp.ones((three.shape[0], tile), BF16), 0, 0)[:hidden]

    w_t = gather(0, hidden)
    cot_t = gather(hidden, hidden)
    bias_t = jnp.concatenate([bias_of(packs_ref[x, at + 2 * hidden : at + size, :]) for x, at in starts], axis=0)
    pre_t = mm(w_t, agg, 1, 1) + bias_t
    grad_t = (cot_t.astype(F32) * slope(pre_t)).astype(BF16)
    back_t = mm(w_t, grad_t, 0, 0).astype(BF16)

    w_mine = pack_ref[0:hidden, :]
    mine_t = mm(w_mine, agg, 1, 1) + bias_of(pack_ref[2 * hidden :, :])
    t = jnp.tanh(SCALE * (mine_t + CUBIC * (mine_t * mine_t * mine_t)))
    act_ref[...] = (mine_t * (0.5 * (1.0 + t))).astype(BF16)
    grad_mine = (pack_ref[hidden : 2 * hidden, :].astype(F32) * slope(mine_t)).astype(BF16)
    wgrad = mm(grad_mine, agg, 1, 0)
    bgrad = mm(jnp.ones((8, tile), BF16), grad_mine, 1, 1)
    bgrad = jnp.concatenate([bgrad, jnp.zeros((8, tile - hidden), F32)], axis=1)

    body = zl_n * rows
    share = hidden // y_n
    assert share <= 8
    out_ref[:, :, :body, :] = jnp.zeros((2, y_n * x_n, body, tile), BF16)
    for y in range(y_n):
        piece = [wgrad[y * share : (y + 1) * share], bgrad]
        if share < 8:
            piece.insert(1, jnp.zeros((8 - share, tile), F32))
        piece = jnp.concatenate(piece, axis=0).astype(BF16)
        for x in range(x_n):
            out_ref[0, y * x_n + x, body:, :] = piece
            out_ref[1, y * x_n + x, body:, :] = piece

    acc = None
    for k in range(0, tiles_ref.shape[0], 2):
        pair = mm(back_t, jnp.concatenate([tiles_ref[k], tiles_ref[k + 1]], axis=1), 1, 0)
        for q, contrib in ((k, pair[:, :tile]), (k + 1, pair[:, tile:])):
            src = src_ref[q]
            if q:
                contrib = contrib + jnp.where(src == src_ref[q - 1], acc, 0.0)
            acc = contrib
            y, zl, c = place(src, zl_n)
            away = jnp.where(c == my_c, 0, 1)
            at = (pl.ds(away, 1), pl.ds(y * x_n, x_n), pl.ds(pl.multiple_of(zl * rows, rows), rows), slice(None))
            out_ref[at] = acc.astype(BF16).reshape(1, x_n, rows, tile)


def plane_sum_kernel(y_n, x_n, in_ref, out_ref):
    my_x = lax.axis_index("x")
    zl_n, zh_n, size, _ = out_ref.shape
    rows = size - EXTRA
    body = zl_n * rows
    total = in_ref[0, :body, :].astype(F32)
    for s in range(1, y_n * x_n):
        total = total + in_ref[s, :body, :].astype(F32)
    extra = in_ref[my_x, body:, :].astype(F32)
    for y in range(1, y_n):
        extra = extra + in_ref[y * x_n + my_x, body:, :].astype(F32)
    total = total.astype(BF16)
    extra = extra.astype(BF16)
    for z in range(zl_n):
        for h in range(zh_n):
            out_ref[z, h, :rows, :] = total[z * rows : (z + 1) * rows]
            out_ref[z, h, rows:, :] = extra


def column_sum_kernel(zl_n, zh_n, in_ref, out_ref):
    my_zh = lax.axis_index("zh")
    rows = in_ref.shape[1] - EXTRA
    total = in_ref[0, :rows, :].astype(F32)
    for s in range(1, zl_n * zh_n):
        total = total + in_ref[s, :rows, :].astype(F32)
    extra = in_ref[my_zh, rows:, :].astype(F32)
    for z in range(1, zl_n):
        extra = extra + in_ref[z * zh_n + my_zh, rows:, :].astype(F32)
    for s in range(out_ref.shape[0]):
        out_ref[s, :rows, :] = total.astype(out_ref.dtype)
        out_ref[s, rows:, :] = extra.astype(out_ref.dtype)


def finish_kernel(y_n, x_n, in_ref, feat_ref, wgrad_ref, bgrad_ref):
    my_x, my_y = lax.axis_index("x"), lax.axis_index("y")
    rows = in_ref.shape[1] - EXTRA
    hidden = bgrad_ref.shape[1]
    share = hidden // y_n
    feat_ref[...] = jnp.concatenate(
        [in_ref[my_y * x_n + x, :rows, :].astype(F32) for x in range(x_n)], axis=0
    ).T
    pieces = [in_ref[y * x_n + my_x, rows:, :].astype(F32) for y in range(y_n)]
    wgrad_ref[...] = jnp.concatenate([p[:share] for p in pieces], axis=0)
    bgrad_ref[...] = pieces[0][8:9, :hidden]


VMEM = pl.BlockSpec(memory_space=pltpu.VMEM)
SMEM = pl.BlockSpec(memory_space=pltpu.SMEM)


def shape(*dims, dtype=BF16):
    return jax.ShapeDtypeStruct(dims, dtype)


def call(kernel, out, *args, smem=0):
    many = isinstance(out, (tuple, list))
    return pl.pallas_call(
        kernel,
        out_shape=out,
        in_specs=[SMEM] * smem + [VMEM] * (len(args) - smem),
        out_specs=[VMEM] * len(out) if many else VMEM,
        compiler_params=PARAMS,
    )(*args)


def to_all(v, axes):
    return lax.all_to_all(v, axes, 0, 0, tiled=True)


def swap(v, axis):
    return lax.ppermute(v, axis, [(0, 1), (1, 0)])


def on_device(sizes, features, tile_values, tile_block, weight, bias, cotangent):
    y_n, zl_n, c_n, x_n, zh_n = (sizes[a] for a in AXES)
    tile = tile_values.shape[-1]
    feat = features.shape[1]
    hidden = bias.shape[0]
    rows = tile // x_n
    tiles = tile_values.reshape(-1, tile, tile)
    sources = tile_block.reshape(-1)
    my_x = lax.axis_index("x")

    b_hi = bias.astype(BF16)
    b_mid = (bias - b_hi.astype(F32)).astype(BF16)
    b_lo = (bias - b_hi.astype(F32) - b_mid.astype(F32)).astype(BF16)
    terms = jnp.pad(jnp.stack([b_hi, b_mid, b_lo]), ((0, 13), (0, feat - hidden)))
    pack = jnp.concatenate([weight.T, cotangent.T, terms], axis=0)
    mine = lax.dynamic_slice_in_dim(features, my_x * rows, rows, 0)
    column = to_all(jnp.broadcast_to(mine[None], (zl_n, rows, feat)), "zl")
    column, pack = lax.optimization_barrier((column, pack))
    pack_other = swap(pack, "zh")
    plane = to_all(jnp.broadcast_to(column[None], (y_n * x_n, zl_n, rows, feat)), ("y", "x"))
    plane, pack_other = lax.optimization_barrier((plane, pack_other))
    own = plane.reshape(y_n, x_n, zl_n, rows, feat)
    other = swap(own, "c")

    size = pack.shape[0]
    part = to_all(
        call(
            functools.partial(forward_kernel, zl_n, x_n),
            shape(x_n, tile + 2 * size, feat),
            sources,
            tiles,
            own,
            other,
            pack,
            pack_other,
            smem=1,
        ),
        "x",
    )
    summed = jnp.sum(part[:, :tile].astype(F32), axis=0).astype(BF16)
    summed_other = swap(summed, "zh")

    act_t, pieces = call(
        functools.partial(backward_kernel, zl_n),
        (shape(hidden, tile), shape(2, y_n * x_n, zl_n * rows + EXTRA, feat)),
        sources,
        summed,
        summed_other,
        part,
        pack,
        tiles,
        smem=1,
    )
    both = (pieces[0].astype(F32) + swap(pieces[1], "c").astype(F32)).astype(BF16)
    across = to_all(both, ("y", "x"))
    up = call(
        functools.partial(plane_sum_kernel, y_n, x_n), shape(zl_n, zh_n, rows + EXTRA, feat), across
    ).reshape(zl_n * zh_n, rows + EXTRA, feat)
    down = to_all(up, ("zl", "zh"))
    last = call(
        functools.partial(column_sum_kernel, zl_n, zh_n), shape(y_n * x_n, rows + EXTRA, feat), down
    )
    feature_grad, wgrad_t, bias_grad = call(
        functools.partial(finish_kernel, y_n, x_n),
        (shape(tile, feat, dtype=F32), shape(hidden, feat, dtype=F32), shape(1, hidden, dtype=F32)),
        to_all(last, ("y", "x")),
    )
    return act_t.T, feature_grad, wgrad_t.T, bias_grad[0]


def split_mesh(mesh, sizes):
    return Mesh(mesh.devices.reshape(tuple(sizes[a] for a in AXES)), AXES)


def solution(mesh, sizes=None):
    sizes = sizes or {"y": 4, "zl": 8, "c": 2, "x": 4, "zh": 2}
    placed = (
        P(BLK, None),
        P(BLK, HID, None, None, None),
        P(BLK, HID, None),
        P(None, HID),
        P(HID),
        P(BLK, HID),
    )
    return jax.shard_map(
        functools.partial(on_device, sizes),
        mesh=split_mesh(mesh, sizes),
        in_specs=placed,
        out_specs=(P(BLK, HID), P(BLK, None), P(None, HID), P(HID)),
        check_vma=False,
    )
```

```python
import functools

import jax
import jax.numpy as jnp
from jax import lax
from jax.experimental import pallas as pl
from jax.experimental.pallas import tpu as pltpu
from jax.sharding import Mesh
from jax.sharding import PartitionSpec as P

BF16 = jnp.bfloat16
F32 = jnp.float32
AXES = ("y", "zl", "c", "x", "zh")
BLK = ("y", "zl", "c")
HID = ("x", "zh")
EXTRA = 16
SCALE = 0.7978845608028654
CUBIC = 0.044715
PARAMS = pltpu.CompilerParams(vmem_limit_bytes=48 * 1024 * 1024)


def mm(a, b, ca, cb):
    return lax.dot_general(a, b, (((ca,), (cb,)), ((), ())), preferred_element_type=F32)


def slope(v):
    t = jnp.tanh(SCALE * (v + CUBIC * (v * v * v)))
    du = SCALE * (1.0 + (3.0 * CUBIC) * (v * v))
    return 0.5 * (1.0 + t) + 0.5 * v * (1.0 - t * t) * du


def dense_kernel(zl_n, src_ref, tiles_ref, out_ref):
    my_c, my_x = lax.axis_index("c"), lax.axis_index("x")
    x_n = out_ref.shape[0]
    out_ref[...] = jnp.zeros_like(out_ref)
    acc = None
    for k in range(tiles_ref.shape[0]):
        src = src_ref[k]
        piece = tiles_ref[k].astype(F32)
        if k:
            piece = piece + jnp.where(src == src_ref[k - 1], acc, 0.0)
        acc = piece
        y, zl, c = src // (2 * zl_n), (src // 2) % zl_n, src % 2
        at = (pl.ds((y + x_n - my_x) % x_n, 1), pl.ds(jnp.where(c == my_c, 0, 1), 1), pl.ds(zl, 1))
        out_ref[at] = acc.astype(BF16)[None, None, None]


def forward_kernel(d0_ref, d1_ref, d2_ref, d3_ref, own_ref, oth_ref, pack_ref, pack_other_ref, a_ref, out_ref):
    tile = d0_ref.shape[-1]
    feat = own_ref.shape[-1]
    size = pack_ref.shape[0]
    zl_n = d0_ref.shape[1]
    acc = jnp.zeros((tile, feat), F32)
    for core, x_ref in ((0, own_ref), (1, oth_ref)):
        for zl in range(zl_n):
            total = d0_ref[core, zl].astype(F32)
            for ref in (d1_ref, d2_ref, d3_ref)[: out_ref.shape[0] - 1]:
                total = total + ref[core, zl].astype(F32)
            total = total.astype(BF16)
            a_ref[core, zl] = total
            acc = acc + mm(total, x_ref[:, zl].reshape(tile, feat), 1, 0)
    part = acc.astype(BF16)
    for x in range(out_ref.shape[0]):
        out_ref[x, :tile, :] = part
        out_ref[x, tile : tile + size, :] = pack_ref[...]
        out_ref[x, tile + size :, :] = pack_other_ref[...]


def backward_kernel(sum_ref, other_ref, packs_ref, pack_ref, a_ref, act_ref, own_ref, oth_ref):
    x_n = packs_ref.shape[0]
    hidden = act_ref.shape[0]
    tile = a_ref.shape[-1]
    zl_n = a_ref.shape[1]
    size = pack_ref.shape[0]
    y_n = own_ref.shape[0]
    rows = tile // y_n
    agg = (sum_ref[...].astype(F32) + other_ref[...].astype(F32)).astype(BF16)
    starts = [(x, tile + z * size) for x in range(x_n) for z in range(2)]

    def gather(start, count):
        return jnp.concatenate([packs_ref[x, at + start : at + start + count, :] for x, at in starts], axis=0)

    def bias_of(three):
        return mm(three, jnp.ones((three.shape[0], tile), BF16), 0, 0)[:hidden]

    w_t = gather(0, hidden)
    cot_t = gather(hidden, hidden)
    bias_t = jnp.concatenate([bias_of(packs_ref[x, at + 2 * hidden : at + size, :]) for x, at in starts], axis=0)
    pre_t = mm(w_t, agg, 1, 1) + bias_t
    grad_t = (cot_t.astype(F32) * slope(pre_t)).astype(BF16)
    back_t = mm(w_t, grad_t, 0, 0).astype(BF16)

    w_mine = pack_ref[0:hidden, :]
    mine_t = mm(w_mine, agg, 1, 1) + bias_of(pack_ref[2 * hidden :, :])
    t = jnp.tanh(SCALE * (mine_t + CUBIC * (mine_t * mine_t * mine_t)))
    act_ref[...] = (mine_t * (0.5 * (1.0 + t))).astype(BF16)
    grad_mine = (pack_ref[hidden : 2 * hidden, :].astype(F32) * slope(mine_t)).astype(BF16)
    wgrad = mm(grad_mine, agg, 1, 0)
    bgrad = mm(jnp.ones((8, tile), BF16), grad_mine, 1, 1)
    bgrad = jnp.concatenate([bgrad, jnp.zeros((8, tile - hidden), F32)], axis=1)

    body = zl_n * rows
    share = hidden // y_n
    assert share <= 8
    for y in range(y_n):
        piece = [wgrad[y * share : (y + 1) * share], bgrad]
        if share < 8:
            piece.insert(1, jnp.zeros((8 - share, tile), F32))
        piece = jnp.concatenate(piece, axis=0).astype(BF16)
        own_ref[y, body:, :] = piece
        oth_ref[y, body:, :] = piece
    for core, out_ref in ((1, oth_ref), (0, own_ref)):
        for zl in range(0, zl_n, 2):
            pair = mm(back_t, jnp.concatenate([a_ref[core, zl], a_ref[core, zl + 1]], axis=1), 1, 0).astype(BF16)
            for y in range(y_n):
                part = pair[y * rows : (y + 1) * rows]
                out_ref[y, zl * rows : (zl + 1) * rows, :] = part[:, :tile]
                out_ref[y, (zl + 1) * rows : (zl + 2) * rows, :] = part[:, tile:]


def plane_sum_kernel(in_ref, out_ref):
    zl_n, zh_n, size, _ = out_ref.shape
    rows = size - EXTRA
    total = in_ref[0].astype(F32)
    for y in range(1, in_ref.shape[0]):
        total = total + in_ref[y].astype(F32)
    total = total.astype(BF16)
    for z in range(zl_n):
        for h in range(zh_n):
            out_ref[z, h, :rows, :] = total[z * rows : (z + 1) * rows]
            out_ref[z, h, rows:, :] = total[zl_n * rows :]


def column_sum_kernel(zl_n, zh_n, in_ref, out_ref):
    my_zh = lax.axis_index("zh")
    rows = in_ref.shape[1] - EXTRA
    total = in_ref[0, :rows, :].astype(F32)
    for s in range(1, zl_n * zh_n):
        total = total + in_ref[s, :rows, :].astype(F32)
    extra = in_ref[my_zh, rows:, :].astype(F32)
    for z in range(1, zl_n):
        extra = extra + in_ref[z * zh_n + my_zh, rows:, :].astype(F32)
    for s in range(out_ref.shape[0]):
        out_ref[s, :rows, :] = total.astype(out_ref.dtype)
        out_ref[s, rows:, :] = extra.astype(out_ref.dtype)


def finish_kernel(y_n, x_n, in_ref, feat_ref, wgrad_ref, bgrad_ref):
    my_x, my_y = lax.axis_index("x"), lax.axis_index("y")
    rows = in_ref.shape[1] - EXTRA
    hidden = bgrad_ref.shape[1]
    share = hidden // y_n
    feat_ref[...] = jnp.concatenate(
        [in_ref[y * x_n + my_y, :rows, :].astype(F32) for y in range(y_n)], axis=0
    ).T
    pieces = [in_ref[y * x_n + my_x, rows:, :].astype(F32) for y in range(y_n)]
    wgrad_ref[...] = jnp.concatenate([p[:share] for p in pieces], axis=0)
    bgrad_ref[...] = pieces[0][8:9, :hidden]


VMEM = pl.BlockSpec(memory_space=pltpu.VMEM)
SMEM = pl.BlockSpec(memory_space=pltpu.SMEM)


def shape(*dims, dtype=BF16):
    return jax.ShapeDtypeStruct(dims, dtype)


def call(kernel, out, *args, smem=0):
    many = isinstance(out, (tuple, list))
    return pl.pallas_call(
        kernel,
        out_shape=out,
        in_specs=[SMEM] * smem + [VMEM] * (len(args) - smem),
        out_specs=[VMEM] * len(out) if many else VMEM,
        compiler_params=PARAMS,
    )(*args)


def to_all(v, axes):
    return lax.all_to_all(v, axes, 0, 0, tiled=True)


def swap(v, axis):
    return lax.ppermute(v, axis, [(0, 1), (1, 0)])


def on_device(sizes, features, tile_values, tile_block, weight, bias, cotangent):
    y_n, zl_n, c_n, x_n, zh_n = (sizes[a] for a in AXES)
    tile = tile_values.shape[-1]
    feat = features.shape[1]
    hidden = bias.shape[0]
    rows = tile // y_n
    tiles = tile_values.reshape(-1, tile, tile)
    sources = tile_block.reshape(-1)
    my_x = lax.axis_index("x")

    b_hi = bias.astype(BF16)
    b_mid = (bias - b_hi.astype(F32)).astype(BF16)
    b_lo = (bias - b_hi.astype(F32) - b_mid.astype(F32)).astype(BF16)
    terms = jnp.pad(jnp.stack([b_hi, b_mid, b_lo]), ((0, 13), (0, feat - hidden)))
    pack = jnp.concatenate([weight.T, cotangent.T, terms], axis=0)
    dense = call(
        functools.partial(dense_kernel, zl_n),
        shape(x_n, c_n, zl_n, tile, tile),
        sources,
        tiles,
        smem=1,
    )

    quarters = to_all(features.reshape(y_n, rows, feat), "y")
    mine = lax.dynamic_index_in_dim(quarters, my_x, 0, keepdims=False)
    mine, dense = lax.optimization_barrier((mine, dense))
    pieces = [dense[0]]
    for step in range(1, x_n):
        pieces.append(lax.ppermute(dense[step], "x", [(x, (x + step) % x_n) for x in range(x_n)]))
    while len(pieces) < 4:
        pieces.append(pieces[0])
    column = to_all(jnp.broadcast_to(mine[None], (zl_n, rows, feat)), "zl")
    column, pack = lax.optimization_barrier((column, pack))
    pack_other = swap(pack, "zh")
    own = to_all(jnp.broadcast_to(column[None], (y_n, zl_n, rows, feat)), "y")
    own, pack_other = lax.optimization_barrier((own, pack_other))
    other = swap(own, "c")

    size = pack.shape[0]
    a_mine, part = call(
        forward_kernel,
        (shape(c_n, zl_n, tile, tile), shape(x_n, tile + 2 * size, feat)),
        *pieces,
        own,
        other,
        pack,
        pack_other,
    )
    part = to_all(part, "x")
    summed = jnp.sum(part[:, :tile].astype(F32), axis=0).astype(BF16)
    summed_other = swap(summed, "zh")

    payload = shape(y_n, zl_n * rows + EXTRA, tile)
    act_t, keep, give = call(
        backward_kernel,
        (shape(hidden, tile), payload, payload),
        summed,
        summed_other,
        part,
        pack,
        a_mine,
    )
    both = (keep.astype(F32) + swap(give, "c").astype(F32)).astype(BF16)
    across = to_all(both, "y")
    up = call(plane_sum_kernel, shape(zl_n, zh_n, rows + EXTRA, feat), across).reshape(
        zl_n * zh_n, rows + EXTRA, feat
    )
    down = to_all(up, ("zl", "zh"))
    last = call(
        functools.partial(column_sum_kernel, zl_n, zh_n), shape(y_n * x_n, rows + EXTRA, feat), down
    )
    feature_grad, wgrad_t, bias_grad = call(
        functools.partial(finish_kernel, y_n, x_n),
        (shape(tile, feat, dtype=F32), shape(hidden, feat, dtype=F32), shape(1, hidden, dtype=F32)),
        to_all(last, ("y", "x")),
    )
    return act_t.T, feature_grad, wgrad_t.T, bias_grad[0]


def split_mesh(mesh, sizes):
    return Mesh(mesh.devices.reshape(tuple(sizes[a] for a in AXES)), AXES)


def solution(mesh, sizes=None):
    sizes = sizes or {"y": 4, "zl": 8, "c": 2, "x": 4, "zh": 2}
    placed = (
        P(BLK, None),
        P(BLK, HID, None, None, None),
        P(BLK, HID, None),
        P(None, HID),
        P(HID),
        P(BLK, HID),
    )
    return jax.shard_map(
        functools.partial(on_device, sizes),
        mesh=split_mesh(mesh, sizes),
        in_specs=placed,
        out_specs=(P(BLK, HID), P(BLK, None), P(None, HID), P(HID)),
        check_vma=False,
    )
```

```python
import functools

import jax
import jax.numpy as jnp
from jax import lax
from jax.experimental import pallas as pl
from jax.experimental.pallas import tpu as pltpu
from jax.sharding import Mesh
from jax.sharding import PartitionSpec as P

BF16 = jnp.bfloat16
F32 = jnp.float32
AXES = ("y", "zl", "c", "x", "zh")
BLK = ("y", "zl", "c")
HID = ("x", "zh")
EXTRA = 16
SCALE = 0.7978845608028654
CUBIC = 0.044715
PARAMS = pltpu.CompilerParams(vmem_limit_bytes=48 * 1024 * 1024)


def mm(a, b, ca, cb):
    return lax.dot_general(a, b, (((ca,), (cb,)), ((), ())), preferred_element_type=F32)


def slope(v):
    t = jnp.tanh(SCALE * (v + CUBIC * (v * v * v)))
    du = SCALE * (1.0 + (3.0 * CUBIC) * (v * v))
    return 0.5 * (1.0 + t) + 0.5 * v * (1.0 - t * t) * du


def dense_kernel(zl_n, src_ref, tiles_ref, out_ref):
    my_c, my_x = lax.axis_index("c"), lax.axis_index("x")
    x_n = out_ref.shape[0]
    out_ref[...] = jnp.zeros_like(out_ref)
    acc = None
    for k in range(tiles_ref.shape[0]):
        src = src_ref[k]
        piece = tiles_ref[k].astype(F32)
        if k:
            piece = piece + jnp.where(src == src_ref[k - 1], acc, 0.0)
        acc = piece
        y, zl, c = src // (2 * zl_n), (src // 2) % zl_n, src % 2
        at = (pl.ds((y + x_n - my_x) % x_n, 1), pl.ds(jnp.where(c == my_c, 0, 1), 1), pl.ds(zl, 1))
        out_ref[at] = acc.astype(BF16)[None, None, None]


def forward_kernel(d0_ref, d1_ref, d2_ref, d3_ref, own_ref, oth_ref, pack_ref, a_ref, out_ref):
    tile = d0_ref.shape[-1]
    feat = own_ref.shape[-1]
    zl_n = d0_ref.shape[1]
    acc = jnp.zeros((tile, feat), F32)
    for core, x_ref in ((0, own_ref), (1, oth_ref)):
        for zl in range(zl_n):
            total = d0_ref[core, zl].astype(F32)
            for ref in (d1_ref, d2_ref, d3_ref)[: out_ref.shape[0] - 1]:
                total = total + ref[core, zl].astype(F32)
            total = total.astype(BF16)
            a_ref[core, zl] = total
            acc = acc + mm(total, x_ref[:, zl].reshape(tile, feat), 1, 0)
    part = acc.astype(BF16)
    for x in range(out_ref.shape[0]):
        out_ref[x, :tile, :] = part
        out_ref[x, tile:, :] = pack_ref[...]


def row_sum_kernel(in_ref, out_ref):
    tile = in_ref.shape[2]
    size = in_ref.shape[1] - tile
    total = in_ref[0, :tile, :].astype(F32)
    for x in range(1, in_ref.shape[0]):
        total = total + in_ref[x, :tile, :].astype(F32)
    out_ref[:tile, :] = total.astype(BF16)
    for x in range(in_ref.shape[0]):
        out_ref[tile + x * size : tile + (x + 1) * size, :] = in_ref[x, tile:, :]


def backward_kernel(sum_ref, other_ref, pack_ref, a_ref, act_ref, own_ref, oth_ref):
    hidden = act_ref.shape[0]
    tile = a_ref.shape[-1]
    zl_n = a_ref.shape[1]
    size = pack_ref.shape[0]
    y_n = own_ref.shape[0]
    rows = tile // y_n
    agg = (sum_ref[:tile, :].astype(F32) + other_ref[:tile, :].astype(F32)).astype(BF16)
    starts = [(ref, at) for at in range(tile, sum_ref.shape[0], size) for ref in (sum_ref, other_ref)]

    def gather(start, count):
        return jnp.concatenate([ref[at + start : at + start + count, :] for ref, at in starts], axis=0)

    def bias_of(three):
        return mm(three, jnp.ones((three.shape[0], tile), BF16), 0, 0)[:hidden]

    w_t = gather(0, hidden)
    cot_t = gather(hidden, hidden)
    bias_t = jnp.concatenate([bias_of(ref[at + 2 * hidden : at + size, :]) for ref, at in starts], axis=0)
    pre_t = mm(w_t, agg, 1, 1) + bias_t
    grad_t = (cot_t.astype(F32) * slope(pre_t)).astype(BF16)
    back_t = mm(w_t, grad_t, 0, 0).astype(BF16)

    w_mine = pack_ref[0:hidden, :]
    mine_t = mm(w_mine, agg, 1, 1) + bias_of(pack_ref[2 * hidden :, :])
    t = jnp.tanh(SCALE * (mine_t + CUBIC * (mine_t * mine_t * mine_t)))
    act_ref[...] = (mine_t * (0.5 * (1.0 + t))).astype(BF16)
    grad_mine = (pack_ref[hidden : 2 * hidden, :].astype(F32) * slope(mine_t)).astype(BF16)
    wgrad = mm(grad_mine, agg, 1, 0)
    bgrad = mm(jnp.ones((8, tile), BF16), grad_mine, 1, 1)
    bgrad = jnp.concatenate([bgrad, jnp.zeros((8, tile - hidden), F32)], axis=1)

    body = zl_n * rows
    share = hidden // y_n
    assert share <= 8
    for y in range(y_n):
        piece = [wgrad[y * share : (y + 1) * share], bgrad]
        if share < 8:
            piece.insert(1, jnp.zeros((8 - share, tile), F32))
        piece = jnp.concatenate(piece, axis=0).astype(BF16)
        own_ref[y, body:, :] = piece
        oth_ref[y, body:, :] = piece
    for core, out_ref in ((1, oth_ref), (0, own_ref)):
        for zl in range(0, zl_n, 2):
            pair = mm(back_t, jnp.concatenate([a_ref[core, zl], a_ref[core, zl + 1]], axis=1), 1, 0).astype(BF16)
            for y in range(y_n):
                part = pair[y * rows : (y + 1) * rows]
                out_ref[y, zl * rows : (zl + 1) * rows, :] = part[:, :tile]
                out_ref[y, (zl + 1) * rows : (zl + 2) * rows, :] = part[:, tile:]


def plane_sum_kernel(in_ref, out_ref):
    zl_n, zh_n, size, _ = out_ref.shape
    rows = size - EXTRA
    total = in_ref[0].astype(F32)
    for y in range(1, in_ref.shape[0]):
        total = total + in_ref[y].astype(F32)
    total = total.astype(BF16)
    for z in range(zl_n):
        for h in range(zh_n):
            out_ref[z, h, :rows, :] = total[z * rows : (z + 1) * rows]
            out_ref[z, h, rows:, :] = total[zl_n * rows :]


def column_sum_kernel(zl_n, zh_n, in_ref, out_ref):
    my_zh = lax.axis_index("zh")
    rows = in_ref.shape[1] - EXTRA
    total = in_ref[0, :rows, :].astype(F32)
    for s in range(1, zl_n * zh_n):
        total = total + in_ref[s, :rows, :].astype(F32)
    extra = in_ref[my_zh, rows:, :].astype(F32)
    for z in range(1, zl_n):
        extra = extra + in_ref[z * zh_n + my_zh, rows:, :].astype(F32)
    for s in range(out_ref.shape[0]):
        out_ref[s, :rows, :] = total.astype(out_ref.dtype)
        out_ref[s, rows:, :] = extra.astype(out_ref.dtype)


def finish_kernel(y_n, x_n, in_ref, feat_ref, wgrad_ref, bgrad_ref):
    my_x, my_y = lax.axis_index("x"), lax.axis_index("y")
    rows = in_ref.shape[1] - EXTRA
    hidden = bgrad_ref.shape[1]
    share = hidden // y_n
    feat_ref[...] = jnp.concatenate(
        [in_ref[y * x_n + my_y, :rows, :].astype(F32) for y in range(y_n)], axis=0
    ).T
    pieces = [in_ref[y * x_n + my_x, rows:, :].astype(F32) for y in range(y_n)]
    wgrad_ref[...] = jnp.concatenate([p[:share] for p in pieces], axis=0)
    bgrad_ref[...] = pieces[0][8:9, :hidden]


VMEM = pl.BlockSpec(memory_space=pltpu.VMEM)
SMEM = pl.BlockSpec(memory_space=pltpu.SMEM)


def shape(*dims, dtype=BF16):
    return jax.ShapeDtypeStruct(dims, dtype)


def call(kernel, out, *args, smem=0):
    many = isinstance(out, (tuple, list))
    return pl.pallas_call(
        kernel,
        out_shape=out,
        in_specs=[SMEM] * smem + [VMEM] * (len(args) - smem),
        out_specs=[VMEM] * len(out) if many else VMEM,
        compiler_params=PARAMS,
    )(*args)


def to_all(v, axes):
    return lax.all_to_all(v, axes, 0, 0, tiled=True)


def swap(v, axis):
    return lax.ppermute(v, axis, [(0, 1), (1, 0)])


def on_device(sizes, features, tile_values, tile_block, weight, bias, cotangent):
    y_n, zl_n, c_n, x_n, zh_n = (sizes[a] for a in AXES)
    tile = tile_values.shape[-1]
    feat = features.shape[1]
    hidden = bias.shape[0]
    rows = tile // y_n
    tiles = tile_values.reshape(-1, tile, tile)
    sources = tile_block.reshape(-1)
    my_x = lax.axis_index("x")

    b_hi = bias.astype(BF16)
    b_mid = (bias - b_hi.astype(F32)).astype(BF16)
    b_lo = (bias - b_hi.astype(F32) - b_mid.astype(F32)).astype(BF16)
    terms = jnp.pad(jnp.stack([b_hi, b_mid, b_lo]), ((0, 13), (0, feat - hidden)))
    pack = jnp.concatenate([weight.T, cotangent.T, terms], axis=0)
    dense = call(
        functools.partial(dense_kernel, zl_n),
        shape(x_n, c_n, zl_n, tile, tile),
        sources,
        tiles,
        smem=1,
    )

    def along_x(v, step):
        return lax.ppermute(v, "x", [(x, (x + step) % x_n) for x in range(x_n)])

    shares = [dense[0], along_x(dense[1], 1)]
    quarters = to_all(features.reshape(y_n, rows, feat), "y")
    mine = lax.dynamic_index_in_dim(quarters, my_x, 0, keepdims=False)
    if x_n > 2:
        mine, second = lax.optimization_barrier((mine, dense[2]))
        shares.append(along_x(second, 2))
    column = to_all(jnp.broadcast_to(mine[None], (zl_n, rows, feat)), "zl")
    if x_n > 3:
        column, third, *shares = lax.optimization_barrier((column, dense[3], *shares))
        shares.append(along_x(third, 3))
    own = to_all(jnp.broadcast_to(column[None], (y_n, zl_n, rows, feat)), "y")
    other = swap(own, "c")

    size = pack.shape[0]
    a_mine, part = call(
        forward_kernel,
        (shape(c_n, zl_n, tile, tile), shape(x_n, tile + size, feat)),
        *(shares + shares)[:4],
        own,
        other,
        pack,
    )
    summed = call(row_sum_kernel, shape(tile + x_n * size, feat), to_all(part, "x"))
    summed_other = swap(summed, "zh")

    payload = shape(y_n, zl_n * rows + EXTRA, tile)
    act_t, keep, give = call(
        backward_kernel,
        (shape(hidden, tile), payload, payload),
        summed,
        summed_other,
        pack,
        a_mine,
    )
    both = (keep.astype(F32) + swap(give, "c").astype(F32)).astype(BF16)
    across = to_all(both, "y")
    up = call(plane_sum_kernel, shape(zl_n, zh_n, rows + EXTRA, feat), across).reshape(
        zl_n * zh_n, rows + EXTRA, feat
    )
    down = to_all(up, ("zl", "zh"))
    last = call(
        functools.partial(column_sum_kernel, zl_n, zh_n), shape(y_n * x_n, rows + EXTRA, feat), down
    )
    feature_grad, wgrad_t, bias_grad = call(
        functools.partial(finish_kernel, y_n, x_n),
        (shape(tile, feat, dtype=F32), shape(hidden, feat, dtype=F32), shape(1, hidden, dtype=F32)),
        to_all(last, ("y", "x")),
    )
    return act_t.T, feature_grad, wgrad_t.T, bias_grad[0]


def split_mesh(mesh, sizes):
    return Mesh(mesh.devices.reshape(tuple(sizes[a] for a in AXES)), AXES)


def solution(mesh, sizes=None):
    sizes = sizes or {"y": 4, "zl": 8, "c": 2, "x": 4, "zh": 2}
    placed = (
        P(BLK, None),
        P(BLK, HID, None, None, None),
        P(BLK, HID, None),
        P(None, HID),
        P(HID),
        P(BLK, HID),
    )
    return jax.shard_map(
        functools.partial(on_device, sizes),
        mesh=split_mesh(mesh, sizes),
        in_specs=placed,
        out_specs=(P(BLK, HID), P(BLK, None), P(None, HID), P(HID)),
        check_vma=False,
    )
```

```python
import functools

import jax
import jax.numpy as jnp
from jax import lax
from jax.experimental import pallas as pl
from jax.experimental.pallas import tpu as pltpu
from jax.sharding import Mesh
from jax.sharding import PartitionSpec as P

BF16 = jnp.bfloat16
F32 = jnp.float32
AXES = ("y", "zl", "c", "x", "zh")
BLK = ("y", "zl", "c")
HID = ("x", "zh")
EXTRA = 16
SCALE = 0.7978845608028654
CUBIC = 0.044715
PARAMS = pltpu.CompilerParams(vmem_limit_bytes=48 * 1024 * 1024)


def mm(a, b, ca, cb):
    return lax.dot_general(a, b, (((ca,), (cb,)), ((), ())), preferred_element_type=F32)


def slope(v):
    t = jnp.tanh(SCALE * (v + CUBIC * (v * v * v)))
    du = SCALE * (1.0 + (3.0 * CUBIC) * (v * v))
    return 0.5 * (1.0 + t) + 0.5 * v * (1.0 - t * t) * du


def dense_kernel(zl_n, src_ref, tiles_ref, out_ref):
    my_c, my_x = lax.axis_index("c"), lax.axis_index("x")
    x_n = out_ref.shape[0]
    out_ref[...] = jnp.zeros_like(out_ref)
    acc = None
    for k in range(tiles_ref.shape[0]):
        src = src_ref[k]
        piece = tiles_ref[k].astype(F32)
        if k:
            piece = piece + jnp.where(src == src_ref[k - 1], acc, 0.0)
        acc = piece
        y, zl, c = src // (2 * zl_n), (src // 2) % zl_n, src % 2
        at = (pl.ds((y + x_n - my_x) % x_n, 1), pl.ds(jnp.where(c == my_c, 0, 1), 1), pl.ds(zl, 1))
        out_ref[at] = acc.astype(BF16)[None, None, None]


def forward_kernel(d0_ref, d1_ref, d2_ref, d3_ref, feat_ref, pack_ref, pack_other_ref, a_ref, out_ref):
    my_c = lax.axis_index("c")
    tile = d0_ref.shape[-1]
    feat = feat_ref.shape[-1]
    size = pack_ref.shape[0]
    zl_n = d0_ref.shape[1]
    acc = jnp.zeros((tile, feat), F32)
    for core in range(2):
        for zl in range(zl_n):
            total = d0_ref[core, zl].astype(F32)
            for ref in (d1_ref, d2_ref, d3_ref)[: out_ref.shape[0] - 1]:
                total = total + ref[core, zl].astype(F32)
            total = total.astype(BF16)
            a_ref[core, zl] = total
            at = (slice(None), pl.ds(my_c if core == 0 else 1 - my_c, 1), slice(zl, zl + 1))
            acc = acc + mm(total, feat_ref[at].reshape(tile, feat), 1, 0)
    part = acc.astype(BF16)
    for x in range(out_ref.shape[0]):
        out_ref[x, :tile, :] = part
        out_ref[x, tile : tile + size, :] = pack_ref[...]
        out_ref[x, tile + size :, :] = pack_other_ref[...]


def backward_kernel(sum_ref, other_ref, packs_ref, pack_ref, a_ref, act_ref, own_ref, oth_ref):
    x_n = packs_ref.shape[0]
    hidden = act_ref.shape[0]
    tile = a_ref.shape[-1]
    zl_n = a_ref.shape[1]
    size = pack_ref.shape[0]
    y_n = own_ref.shape[0]
    rows = tile // y_n
    agg = (sum_ref[...].astype(F32) + other_ref[...].astype(F32)).astype(BF16)
    starts = [(x, tile + z * size) for x in range(x_n) for z in range(2)]

    def gather(start, count):
        return jnp.concatenate([packs_ref[x, at + start : at + start + count, :] for x, at in starts], axis=0)

    def bias_of(three):
        return mm(three, jnp.ones((three.shape[0], tile), BF16), 0, 0)[:hidden]

    w_t = gather(0, hidden)
    cot_t = gather(hidden, hidden)
    bias_t = jnp.concatenate([bias_of(packs_ref[x, at + 2 * hidden : at + size, :]) for x, at in starts], axis=0)
    pre_t = mm(w_t, agg, 1, 1) + bias_t
    grad_t = (cot_t.astype(F32) * slope(pre_t)).astype(BF16)
    back_t = mm(w_t, grad_t, 0, 0).astype(BF16)

    w_mine = pack_ref[0:hidden, :]
    mine_t = mm(w_mine, agg, 1, 1) + bias_of(pack_ref[2 * hidden :, :])
    t = jnp.tanh(SCALE * (mine_t + CUBIC * (mine_t * mine_t * mine_t)))
    act_ref[...] = (mine_t * (0.5 * (1.0 + t))).astype(BF16)
    grad_mine = (pack_ref[hidden : 2 * hidden, :].astype(F32) * slope(mine_t)).astype(BF16)
    wgrad = mm(grad_mine, agg, 1, 0)
    bgrad = mm(jnp.ones((8, tile), BF16), grad_mine, 1, 1)
    bgrad = jnp.concatenate([bgrad, jnp.zeros((8, tile - hidden), F32)], axis=1)

    body = zl_n * rows
    share = hidden // y_n
    assert share <= 8
    for y in range(y_n):
        piece = [wgrad[y * share : (y + 1) * share], bgrad]
        if share < 8:
            piece.insert(1, jnp.zeros((8 - share, tile), F32))
        piece = jnp.concatenate(piece, axis=0).astype(BF16)
        own_ref[y, body:, :] = piece
        oth_ref[y, body:, :] = piece
    for core, out_ref in ((1, oth_ref), (0, own_ref)):
        for zl in range(0, zl_n, 2):
            pair = mm(back_t, jnp.concatenate([a_ref[core, zl], a_ref[core, zl + 1]], axis=1), 1, 0).astype(BF16)
            for y in range(y_n):
                part = pair[y * rows : (y + 1) * rows]
                out_ref[y, zl * rows : (zl + 1) * rows, :] = part[:, :tile]
                out_ref[y, (zl + 1) * rows : (zl + 2) * rows, :] = part[:, tile:]


def plane_sum_kernel(in_ref, out_ref):
    zl_n, zh_n, size, _ = out_ref.shape
    rows = size - EXTRA
    total = in_ref[0].astype(F32)
    for y in range(1, in_ref.shape[0]):
        total = total + in_ref[y].astype(F32)
    total = total.astype(BF16)
    for z in range(zl_n):
        for h in range(zh_n):
            out_ref[z, h, :rows, :] = total[z * rows : (z + 1) * rows]
            out_ref[z, h, rows:, :] = total[zl_n * rows :]


def column_sum_kernel(zl_n, zh_n, in_ref, out_ref):
    my_zh = lax.axis_index("zh")
    rows = in_ref.shape[1] - EXTRA
    total = in_ref[0, :rows, :].astype(F32)
    for s in range(1, zl_n * zh_n):
        total = total + in_ref[s, :rows, :].astype(F32)
    extra = in_ref[my_zh, rows:, :].astype(F32)
    for z in range(1, zl_n):
        extra = extra + in_ref[z * zh_n + my_zh, rows:, :].astype(F32)
    for s in range(out_ref.shape[0]):
        out_ref[s, :rows, :] = total.astype(out_ref.dtype)
        out_ref[s, rows:, :] = extra.astype(out_ref.dtype)


def finish_kernel(y_n, x_n, in_ref, feat_ref, wgrad_ref, bgrad_ref):
    my_x, my_y = lax.axis_index("x"), lax.axis_index("y")
    rows = in_ref.shape[1] - EXTRA
    hidden = bgrad_ref.shape[1]
    share = hidden // y_n
    feat_ref[...] = jnp.concatenate(
        [in_ref[y * x_n + my_y, :rows, :].astype(F32) for y in range(y_n)], axis=0
    ).T
    pieces = [in_ref[y * x_n + my_x, rows:, :].astype(F32) for y in range(y_n)]
    wgrad_ref[...] = jnp.concatenate([p[:share] for p in pieces], axis=0)
    bgrad_ref[...] = pieces[0][8:9, :hidden]


VMEM = pl.BlockSpec(memory_space=pltpu.VMEM)
SMEM = pl.BlockSpec(memory_space=pltpu.SMEM)


def shape(*dims, dtype=BF16):
    return jax.ShapeDtypeStruct(dims, dtype)


def call(kernel, out, *args, smem=0):
    many = isinstance(out, (tuple, list))
    return pl.pallas_call(
        kernel,
        out_shape=out,
        in_specs=[SMEM] * smem + [VMEM] * (len(args) - smem),
        out_specs=[VMEM] * len(out) if many else VMEM,
        compiler_params=PARAMS,
    )(*args)


def to_all(v, axes):
    return lax.all_to_all(v, axes, 0, 0, tiled=True)


def swap(v, axis):
    return lax.ppermute(v, axis, [(0, 1), (1, 0)])


def on_device(sizes, features, tile_values, tile_block, weight, bias, cotangent):
    y_n, zl_n, c_n, x_n, zh_n = (sizes[a] for a in AXES)
    tile = tile_values.shape[-1]
    feat = features.shape[1]
    hidden = bias.shape[0]
    rows = tile // y_n
    tiles = tile_values.reshape(-1, tile, tile)
    sources = tile_block.reshape(-1)
    my_x = lax.axis_index("x")

    b_hi = bias.astype(BF16)
    b_mid = (bias - b_hi.astype(F32)).astype(BF16)
    b_lo = (bias - b_hi.astype(F32) - b_mid.astype(F32)).astype(BF16)
    terms = jnp.pad(jnp.stack([b_hi, b_mid, b_lo]), ((0, 13), (0, feat - hidden)))
    pack = jnp.concatenate([weight.T, cotangent.T, terms], axis=0)
    dense = call(
        functools.partial(dense_kernel, zl_n),
        shape(x_n, c_n, zl_n, tile, tile),
        sources,
        tiles,
        smem=1,
    )

    quarters = to_all(features.reshape(y_n, rows, feat), "y")
    mine = lax.dynamic_index_in_dim(quarters, my_x, 0, keepdims=False)
    mine, dense = lax.optimization_barrier((mine, dense))
    pieces = [dense[0]]
    for step in range(1, x_n):
        pieces.append(lax.ppermute(dense[step], "x", [(x, (x + step) % x_n) for x in range(x_n)]))
    while len(pieces) < 4:
        pieces.append(pieces[0])
    column = to_all(jnp.broadcast_to(mine[None], (zl_n, rows, feat)), "zl")
    column = lax.all_gather(column, "c")
    column, pack = lax.optimization_barrier((column, pack))
    pack_other = swap(pack, "zh")
    blocks = to_all(jnp.broadcast_to(column[None], (y_n,) + column.shape), "y")

    size = pack.shape[0]
    a_mine, part = call(
        forward_kernel,
        (shape(c_n, zl_n, tile, tile), shape(x_n, tile + 2 * size, feat)),
        *pieces,
        blocks,
        pack,
        pack_other,
    )
    part = to_all(part, "x")
    summed = jnp.sum(part[:, :tile].astype(F32), axis=0).astype(BF16)
    summed_other = swap(summed, "zh")

    payload = shape(y_n, zl_n * rows + EXTRA, tile)
    act_t, keep, give = call(
        backward_kernel,
        (shape(hidden, tile), payload, payload),
        summed,
        summed_other,
        part,
        pack,
        a_mine,
    )
    both = (keep.astype(F32) + swap(give, "c").astype(F32)).astype(BF16)
    across = to_all(both, "y")
    up = call(plane_sum_kernel, shape(zl_n, zh_n, rows + EXTRA, feat), across).reshape(
        zl_n * zh_n, rows + EXTRA, feat
    )
    down = to_all(up, ("zl", "zh"))
    last = call(
        functools.partial(column_sum_kernel, zl_n, zh_n), shape(y_n * x_n, rows + EXTRA, feat), down
    )
    feature_grad, wgrad_t, bias_grad = call(
        functools.partial(finish_kernel, y_n, x_n),
        (shape(tile, feat, dtype=F32), shape(hidden, feat, dtype=F32), shape(1, hidden, dtype=F32)),
        to_all(last, ("y", "x")),
    )
    return act_t.T, feature_grad, wgrad_t.T, bias_grad[0]


def split_mesh(mesh, sizes):
    return Mesh(mesh.devices.reshape(tuple(sizes[a] for a in AXES)), AXES)


def solution(mesh, sizes=None):
    sizes = sizes or {"y": 4, "zl": 8, "c": 2, "x": 4, "zh": 2}
    placed = (
        P(BLK, None),
        P(BLK, HID, None, None, None),
        P(BLK, HID, None),
        P(None, HID),
        P(HID),
        P(BLK, HID),
    )
    return jax.shard_map(
        functools.partial(on_device, sizes),
        mesh=split_mesh(mesh, sizes),
        in_specs=placed,
        out_specs=(P(BLK, HID), P(BLK, None), P(None, HID), P(HID)),
        check_vma=False,
    )
```

```python
import functools

import jax
import jax.numpy as jnp
from jax import lax
from jax.experimental import pallas as pl
from jax.experimental.pallas import tpu as pltpu
from jax.sharding import Mesh
from jax.sharding import PartitionSpec as P

BF16 = jnp.bfloat16
F32 = jnp.float32
AXES = ("y", "zl", "c", "x", "zh")
BLK = ("y", "zl", "c")
HID = ("x", "zh")
EXTRA = 16
SCALE = 0.7978845608028654
CUBIC = 0.044715
PARAMS = pltpu.CompilerParams(vmem_limit_bytes=48 * 1024 * 1024)


def mm(a, b, ca, cb):
    return lax.dot_general(a, b, (((ca,), (cb,)), ((), ())), preferred_element_type=F32)


def slope(v):
    t = jnp.tanh(SCALE * (v + CUBIC * (v * v * v)))
    du = SCALE * (1.0 + (3.0 * CUBIC) * (v * v))
    return 0.5 * (1.0 + t) + 0.5 * v * (1.0 - t * t) * du


def dense_kernel(zl_n, src_ref, tiles_ref, out_ref):
    my_c, my_x = lax.axis_index("c"), lax.axis_index("x")
    x_n = out_ref.shape[0]
    out_ref[...] = jnp.zeros_like(out_ref)
    acc = None
    for k in range(tiles_ref.shape[0]):
        src = src_ref[k]
        piece = tiles_ref[k].astype(F32)
        if k:
            piece = piece + jnp.where(src == src_ref[k - 1], acc, 0.0)
        acc = piece
        y, zl, c = src // (2 * zl_n), (src // 2) % zl_n, src % 2
        at = (pl.ds((y + x_n - my_x) % x_n, 1), pl.ds(jnp.where(c == my_c, 0, 1), 1), pl.ds(zl, 1))
        out_ref[at] = acc.astype(BF16)[None, None, None]


def forward_kernel(d0_ref, d1_ref, d2_ref, d3_ref, feat_ref, pack_ref, a_ref, out_ref):
    my_c = lax.axis_index("c")
    tile = d0_ref.shape[-1]
    feat = feat_ref.shape[-1]
    zl_n = d0_ref.shape[1]
    acc = jnp.zeros((tile, feat), F32)
    for core in range(2):
        for zl in range(zl_n):
            total = d0_ref[core, zl].astype(F32)
            for ref in (d1_ref, d2_ref, d3_ref)[: out_ref.shape[0] - 1]:
                total = total + ref[core, zl].astype(F32)
            total = total.astype(BF16)
            a_ref[core, zl] = total
            at = (slice(None), pl.ds(my_c if core == 0 else 1 - my_c, 1), slice(zl, zl + 1))
            acc = acc + mm(total, feat_ref[at].reshape(tile, feat), 1, 0)
    part = acc.astype(BF16)
    for x in range(out_ref.shape[0]):
        out_ref[x, :tile, :] = part
        out_ref[x, tile:, :] = pack_ref[...]


def row_sum_kernel(hidden, in_ref, out_ref):
    tile = in_ref.shape[2]
    x_n = in_ref.shape[0]
    size = 2 * hidden
    total = in_ref[0, :tile, :].astype(F32)
    for x in range(1, x_n):
        total = total + in_ref[x, :tile, :].astype(F32)
    out_ref[:tile, :] = total.astype(BF16)
    for x in range(x_n):
        out_ref[tile + x * size : tile + (x + 1) * size, :] = in_ref[x, tile : tile + size, :]
    terms = [in_ref[x, tile + size :, :].astype(F32)[:4] for x in range(x_n)]
    terms = jnp.concatenate(terms + [jnp.zeros((16 - 4 * x_n, tile), F32)] * (x_n < 4), axis=0)
    out_ref[tile + x_n * size :, :] = terms.astype(BF16)


def backward_kernel(x_n, sum_ref, other_ref, pack_ref, a_ref, act_ref, own_ref, oth_ref):
    hidden = act_ref.shape[0]
    tile = a_ref.shape[-1]
    zl_n = a_ref.shape[1]
    y_n = own_ref.shape[0]
    rows = tile // y_n
    agg = (sum_ref[:tile, :].astype(F32) + other_ref[:tile, :].astype(F32)).astype(BF16)

    def gather(start, count):
        parts = [
            ref[tile + x * 2 * hidden + start : tile + x * 2 * hidden + start + count, :]
            for ref in (sum_ref, other_ref)
            for x in range(x_n)
        ]
        return jnp.concatenate(parts, axis=0)

    def bias_of(three):
        return mm(three, jnp.ones((three.shape[0], tile), BF16), 0, 0)[:hidden]

    def biases(ref):
        terms = ref[tile + x_n * 2 * hidden :, :].astype(F32)
        return [bias_of(terms[4 * x : 4 * x + 4].astype(BF16)) for x in range(x_n)]

    w_t = gather(0, hidden)
    cot_t = gather(hidden, hidden)
    bias_t = jnp.concatenate(biases(sum_ref) + biases(other_ref), axis=0)
    pre_t = mm(w_t, agg, 1, 1) + bias_t
    grad_t = (cot_t.astype(F32) * slope(pre_t)).astype(BF16)
    back_t = mm(w_t, grad_t, 0, 0).astype(BF16)

    w_mine = pack_ref[0:hidden, :]
    mine_t = mm(w_mine, agg, 1, 1) + bias_of(pack_ref[2 * hidden :, :])
    t = jnp.tanh(SCALE * (mine_t + CUBIC * (mine_t * mine_t * mine_t)))
    act_ref[...] = (mine_t * (0.5 * (1.0 + t))).astype(BF16)
    grad_mine = (pack_ref[hidden : 2 * hidden, :].astype(F32) * slope(mine_t)).astype(BF16)
    wgrad = mm(grad_mine, agg, 1, 0)
    bgrad = mm(jnp.ones((8, tile), BF16), grad_mine, 1, 1)
    bgrad = jnp.concatenate([bgrad, jnp.zeros((8, tile - hidden), F32)], axis=1)

    body = zl_n * rows
    share = hidden // y_n
    assert share <= 8
    for y in range(y_n):
        piece = [wgrad[y * share : (y + 1) * share], bgrad]
        if share < 8:
            piece.insert(1, jnp.zeros((8 - share, tile), F32))
        piece = jnp.concatenate(piece, axis=0).astype(BF16)
        own_ref[y, body:, :] = piece
        oth_ref[y, body:, :] = piece
    for core, out_ref in ((1, oth_ref), (0, own_ref)):
        for zl in range(0, zl_n, 2):
            pair = mm(back_t, jnp.concatenate([a_ref[core, zl], a_ref[core, zl + 1]], axis=1), 1, 0).astype(BF16)
            for y in range(y_n):
                part = pair[y * rows : (y + 1) * rows]
                out_ref[y, zl * rows : (zl + 1) * rows, :] = part[:, :tile]
                out_ref[y, (zl + 1) * rows : (zl + 2) * rows, :] = part[:, tile:]


def plane_sum_kernel(in_ref, out_ref):
    zl_n, zh_n, size, _ = out_ref.shape
    rows = size - EXTRA
    total = in_ref[0].astype(F32)
    for y in range(1, in_ref.shape[0]):
        total = total + in_ref[y].astype(F32)
    total = total.astype(BF16)
    for z in range(zl_n):
        for h in range(zh_n):
            out_ref[z, h, :rows, :] = total[z * rows : (z + 1) * rows]
            out_ref[z, h, rows:, :] = total[zl_n * rows :]


def column_sum_kernel(zl_n, zh_n, in_ref, out_ref):
    my_zh = lax.axis_index("zh")
    rows = in_ref.shape[1] - EXTRA
    total = in_ref[0, :rows, :].astype(F32)
    for s in range(1, zl_n * zh_n):
        total = total + in_ref[s, :rows, :].astype(F32)
    extra = in_ref[my_zh, rows:, :].astype(F32)
    for z in range(1, zl_n):
        extra = extra + in_ref[z * zh_n + my_zh, rows:, :].astype(F32)
    for s in range(out_ref.shape[0]):
        out_ref[s, :rows, :] = total.astype(out_ref.dtype)
        out_ref[s, rows:, :] = extra.astype(out_ref.dtype)


def finish_kernel(y_n, x_n, in_ref, feat_ref, wgrad_ref, bgrad_ref):
    my_x, my_y = lax.axis_index("x"), lax.axis_index("y")
    rows = in_ref.shape[1] - EXTRA
    hidden = bgrad_ref.shape[1]
    share = hidden // y_n
    feat_ref[...] = jnp.concatenate(
        [in_ref[y * x_n + my_y, :rows, :].astype(F32) for y in range(y_n)], axis=0
    ).T
    pieces = [in_ref[y * x_n + my_x, rows:, :].astype(F32) for y in range(y_n)]
    wgrad_ref[...] = jnp.concatenate([p[:share] for p in pieces], axis=0)
    bgrad_ref[...] = pieces[0][8:9, :hidden]


VMEM = pl.BlockSpec(memory_space=pltpu.VMEM)
SMEM = pl.BlockSpec(memory_space=pltpu.SMEM)


def shape(*dims, dtype=BF16):
    return jax.ShapeDtypeStruct(dims, dtype)


def call(kernel, out, *args, smem=0):
    many = isinstance(out, (tuple, list))
    return pl.pallas_call(
        kernel,
        out_shape=out,
        in_specs=[SMEM] * smem + [VMEM] * (len(args) - smem),
        out_specs=[VMEM] * len(out) if many else VMEM,
        compiler_params=PARAMS,
    )(*args)


def to_all(v, axes):
    return lax.all_to_all(v, axes, 0, 0, tiled=True)


def swap(v, axis):
    return lax.ppermute(v, axis, [(0, 1), (1, 0)])


def on_device(sizes, features, tile_values, tile_block, weight, bias, cotangent):
    y_n, zl_n, c_n, x_n, zh_n = (sizes[a] for a in AXES)
    tile = tile_values.shape[-1]
    feat = features.shape[1]
    hidden = bias.shape[0]
    rows = tile // y_n
    tiles = tile_values.reshape(-1, tile, tile)
    sources = tile_block.reshape(-1)
    my_x = lax.axis_index("x")

    b_hi = bias.astype(BF16)
    b_mid = (bias - b_hi.astype(F32)).astype(BF16)
    b_lo = (bias - b_hi.astype(F32) - b_mid.astype(F32)).astype(BF16)
    terms = jnp.pad(jnp.stack([b_hi, b_mid, b_lo]), ((0, 13), (0, feat - hidden)))
    pack = jnp.concatenate([weight.T, cotangent.T, terms], axis=0)
    dense = call(
        functools.partial(dense_kernel, zl_n),
        shape(x_n, c_n, zl_n, tile, tile),
        sources,
        tiles,
        smem=1,
    )

    quarters = to_all(features.reshape(y_n, rows, feat), "y")
    mine = lax.dynamic_index_in_dim(quarters, my_x, 0, keepdims=False)
    mine, dense = lax.optimization_barrier((mine, dense))
    pieces = [dense[0]]
    for step in range(1, x_n):
        pieces.append(lax.ppermute(dense[step], "x", [(x, (x + step) % x_n) for x in range(x_n)]))
    while len(pieces) < 4:
        pieces.append(pieces[0])
    column = to_all(jnp.broadcast_to(mine[None], (zl_n, rows, feat)), "zl")
    column = lax.all_gather(column, "c")
    blocks = to_all(jnp.broadcast_to(column[None], (y_n,) + column.shape), "y")

    a_mine, part = call(
        forward_kernel,
        (shape(c_n, zl_n, tile, tile), shape(x_n, tile + pack.shape[0], feat)),
        *pieces,
        blocks,
        pack,
    )
    summed = call(
        functools.partial(row_sum_kernel, hidden),
        shape(tile + x_n * 2 * hidden + 16, feat),
        to_all(part, "x"),
    )
    summed_other = swap(summed, "zh")

    payload = shape(y_n, zl_n * rows + EXTRA, tile)
    act_t, keep, give = call(
        functools.partial(backward_kernel, x_n),
        (shape(hidden, tile), payload, payload),
        summed,
        summed_other,
        pack,
        a_mine,
    )
    both = (keep.astype(F32) + swap(give, "c").astype(F32)).astype(BF16)
    across = to_all(both, "y")
    up = call(plane_sum_kernel, shape(zl_n, zh_n, rows + EXTRA, feat), across).reshape(
        zl_n * zh_n, rows + EXTRA, feat
    )
    down = to_all(up, ("zl", "zh"))
    last = call(
        functools.partial(column_sum_kernel, zl_n, zh_n), shape(y_n * x_n, rows + EXTRA, feat), down
    )
    feature_grad, wgrad_t, bias_grad = call(
        functools.partial(finish_kernel, y_n, x_n),
        (shape(tile, feat, dtype=F32), shape(hidden, feat, dtype=F32), shape(1, hidden, dtype=F32)),
        to_all(last, ("y", "x")),
    )
    return act_t.T, feature_grad, wgrad_t.T, bias_grad[0]


def split_mesh(mesh, sizes):
    return Mesh(mesh.devices.reshape(tuple(sizes[a] for a in AXES)), AXES)


def solution(mesh, sizes=None):
    sizes = sizes or {"y": 4, "zl": 8, "c": 2, "x": 4, "zh": 2}
    placed = (
        P(BLK, None),
        P(BLK, HID, None, None, None),
        P(BLK, HID, None),
        P(None, HID),
        P(HID),
        P(BLK, HID),
    )
    return jax.shard_map(
        functools.partial(on_device, sizes),
        mesh=split_mesh(mesh, sizes),
        in_specs=placed,
        out_specs=(P(BLK, HID), P(BLK, None), P(None, HID), P(HID)),
        check_vma=False,
    )
```

```python
import functools

import jax
import jax.numpy as jnp
from jax import lax
from jax.experimental import pallas as pl
from jax.experimental.pallas import tpu as pltpu
from jax.sharding import Mesh
from jax.sharding import PartitionSpec as P

BF16 = jnp.bfloat16
F32 = jnp.float32
AXES = ("y", "zl", "c", "x", "zh")
BLK = ("y", "zl", "c")
HID = ("x", "zh")
EXTRA = 16
SCALE = 0.7978845608028654
CUBIC = 0.044715
PARAMS = pltpu.CompilerParams(vmem_limit_bytes=48 * 1024 * 1024)


def mm(a, b, ca, cb):
    return lax.dot_general(a, b, (((ca,), (cb,)), ((), ())), preferred_element_type=F32)


def slope(v):
    t = jnp.tanh(SCALE * (v + CUBIC * (v * v * v)))
    du = SCALE * (1.0 + (3.0 * CUBIC) * (v * v))
    return 0.5 * (1.0 + t) + 0.5 * v * (1.0 - t * t) * du


def dense_kernel(zl_n, src_ref, tiles_ref, out_ref):
    my_c, my_x = lax.axis_index("c"), lax.axis_index("x")
    x_n = out_ref.shape[0]
    out_ref[...] = jnp.zeros_like(out_ref)
    acc = None
    for k in range(tiles_ref.shape[0]):
        src = src_ref[k]
        piece = tiles_ref[k].astype(F32)
        if k:
            piece = piece + jnp.where(src == src_ref[k - 1], acc, 0.0)
        acc = piece
        y, zl, c = src // (2 * zl_n), (src // 2) % zl_n, src % 2
        at = (pl.ds((y + x_n - my_x) % x_n, 1), pl.ds(jnp.where(c == my_c, 0, 1), 1), pl.ds(zl, 1))
        out_ref[at] = acc.astype(BF16)[None, None, None]


def forward_kernel(d0_ref, d1_ref, d2_ref, d3_ref, feat_ref, pack_ref, a_ref, out_ref):
    my_c = lax.axis_index("c")
    tile = d0_ref.shape[-1]
    feat = feat_ref.shape[-1]
    zl_n = d0_ref.shape[1]
    acc = jnp.zeros((tile, feat), F32)
    for core in range(2):
        for zl in range(zl_n):
            total = d0_ref[core, zl].astype(F32)
            for ref in (d1_ref, d2_ref, d3_ref)[: out_ref.shape[0] - 1]:
                total = total + ref[core, zl].astype(F32)
            total = total.astype(BF16)
            a_ref[core, zl] = total
            at = (slice(None), pl.ds(my_c if core == 0 else 1 - my_c, 1), slice(zl, zl + 1))
            acc = acc + mm(total, feat_ref[at].reshape(tile, feat), 1, 0)
    part = acc.astype(BF16)
    for x in range(out_ref.shape[0]):
        out_ref[x, :tile, :] = part
        out_ref[x, tile:, :] = pack_ref[...]


def row_sum_kernel(hidden, in_ref, out_ref):
    tile = in_ref.shape[2]
    x_n = in_ref.shape[0]
    size = 2 * hidden
    total = in_ref[0, :tile, :].astype(F32)
    for x in range(1, x_n):
        total = total + in_ref[x, :tile, :].astype(F32)
    out_ref[:tile, :] = total.astype(BF16)
    for x in range(x_n):
        out_ref[tile + x * size : tile + (x + 1) * size, :] = in_ref[x, tile : tile + size, :]
    terms = [in_ref[x, tile + size :, :].astype(F32)[:4] for x in range(x_n)]
    terms = jnp.concatenate(terms + [jnp.zeros((16 - 4 * x_n, tile), F32)] * (x_n < 4), axis=0)
    out_ref[tile + x_n * size :, :] = terms.astype(BF16)


def backward_kernel(x_n, sum_ref, other_ref, pack_ref, a_ref, act_ref, own_ref, oth_ref):
    hidden = act_ref.shape[0]
    tile = a_ref.shape[-1]
    zl_n = a_ref.shape[1]
    y_n = own_ref.shape[0]
    rows = tile // y_n
    agg = (sum_ref[:tile, :].astype(F32) + other_ref[:tile, :].astype(F32)).astype(BF16)

    def gather(start, count):
        parts = [
            ref[tile + x * 2 * hidden + start : tile + x * 2 * hidden + start + count, :]
            for ref in (sum_ref, other_ref)
            for x in range(x_n)
        ]
        return jnp.concatenate(parts, axis=0)

    def bias_of(three):
        return mm(three, jnp.ones((three.shape[0], tile), BF16), 0, 0)[:hidden]

    def biases(ref):
        terms = ref[tile + x_n * 2 * hidden :, :].astype(F32)
        return [bias_of(terms[4 * x : 4 * x + 4].astype(BF16)) for x in range(x_n)]

    w_t = gather(0, hidden)
    cot_t = gather(hidden, hidden)
    bias_t = jnp.concatenate(biases(sum_ref) + biases(other_ref), axis=0)
    pre_t = mm(w_t, agg, 1, 1) + bias_t
    grad_t = (cot_t.astype(F32) * slope(pre_t)).astype(BF16)
    back_t = mm(w_t, grad_t, 0, 0).astype(BF16)

    w_mine = pack_ref[0:hidden, :]
    mine_t = mm(w_mine, agg, 1, 1) + bias_of(pack_ref[2 * hidden :, :])
    t = jnp.tanh(SCALE * (mine_t + CUBIC * (mine_t * mine_t * mine_t)))
    act_ref[...] = (mine_t * (0.5 * (1.0 + t))).astype(BF16)
    grad_mine = (pack_ref[hidden : 2 * hidden, :].astype(F32) * slope(mine_t)).astype(BF16)
    wgrad = mm(grad_mine, agg, 1, 0)
    bgrad = mm(jnp.ones((8, tile), BF16), grad_mine, 1, 1)
    bgrad = jnp.concatenate([bgrad, jnp.zeros((8, tile - hidden), F32)], axis=1)

    body = zl_n * rows
    share = hidden // y_n
    assert share <= 8
    for y in range(y_n):
        piece = [wgrad[y * share : (y + 1) * share], bgrad]
        if share < 8:
            piece.insert(1, jnp.zeros((8 - share, tile), F32))
        piece = jnp.concatenate(piece, axis=0).astype(BF16)
        own_ref[y, body:, :] = piece
        oth_ref[y, body:, :] = piece
    for core, out_ref in ((1, oth_ref), (0, own_ref)):
        for zl in range(0, zl_n, 2):
            pair = mm(back_t, jnp.concatenate([a_ref[core, zl], a_ref[core, zl + 1]], axis=1), 1, 0).astype(BF16)
            for y in range(y_n):
                part = pair[y * rows : (y + 1) * rows]
                out_ref[y, zl * rows : (zl + 1) * rows, :] = part[:, :tile]
                out_ref[y, (zl + 1) * rows : (zl + 2) * rows, :] = part[:, tile:]


def plane_sum_kernel(in_ref, out_ref):
    zl_n, zh_n, size, _ = out_ref.shape
    rows = size - EXTRA
    total = in_ref[0].astype(F32)
    for y in range(1, in_ref.shape[0]):
        total = total + in_ref[y].astype(F32)
    total = total.astype(BF16)
    for z in range(zl_n):
        for h in range(zh_n):
            out_ref[z, h, :rows, :] = total[z * rows : (z + 1) * rows]
            out_ref[z, h, rows:, :] = total[zl_n * rows :]


def column_sum_kernel(zl_n, zh_n, in_ref, out_ref):
    my_zh = lax.axis_index("zh")
    rows = in_ref.shape[1] - EXTRA
    total = in_ref[0, :rows, :].astype(F32)
    for s in range(1, zl_n * zh_n):
        total = total + in_ref[s, :rows, :].astype(F32)
    extra = in_ref[my_zh, rows:, :].astype(F32)
    for z in range(1, zl_n):
        extra = extra + in_ref[z * zh_n + my_zh, rows:, :].astype(F32)
    for s in range(out_ref.shape[0]):
        out_ref[s, :rows, :] = total.astype(out_ref.dtype)
        out_ref[s, rows:, :] = extra.astype(out_ref.dtype)


def finish_kernel(y_n, x_n, in_ref, feat_ref, wgrad_ref, bgrad_ref):
    my_x, my_y = lax.axis_index("x"), lax.axis_index("y")
    rows = in_ref.shape[1] - EXTRA
    hidden = bgrad_ref.shape[1]
    share = hidden // y_n
    feat_ref[...] = jnp.concatenate(
        [in_ref[y * x_n + my_y, :rows, :].astype(F32) for y in range(y_n)], axis=0
    ).T
    pieces = [in_ref[y * x_n + my_x, rows:, :].astype(F32) for y in range(y_n)]
    wgrad_ref[...] = jnp.concatenate([p[:share] for p in pieces], axis=0)
    bgrad_ref[...] = pieces[0][8:9, :hidden]


VMEM = pl.BlockSpec(memory_space=pltpu.VMEM)
SMEM = pl.BlockSpec(memory_space=pltpu.SMEM)


def shape(*dims, dtype=BF16):
    return jax.ShapeDtypeStruct(dims, dtype)


def call(kernel, out, *args, smem=0):
    many = isinstance(out, (tuple, list))
    return pl.pallas_call(
        kernel,
        out_shape=out,
        in_specs=[SMEM] * smem + [VMEM] * (len(args) - smem),
        out_specs=[VMEM] * len(out) if many else VMEM,
        compiler_params=PARAMS,
    )(*args)


def to_all(v, axes):
    return lax.all_to_all(v, axes, 0, 0, tiled=True)


def swap(v, axis):
    return lax.ppermute(v, axis, [(0, 1), (1, 0)])


def on_device(sizes, features, tile_values, tile_block, weight, bias, cotangent):
    y_n, zl_n, c_n, x_n, zh_n = (sizes[a] for a in AXES)
    tile = tile_values.shape[-1]
    feat = features.shape[1]
    hidden = bias.shape[0]
    rows = tile // y_n
    tiles = tile_values.reshape(-1, tile, tile)
    sources = tile_block.reshape(-1)
    my_x = lax.axis_index("x")

    b_hi = bias.astype(BF16)
    b_mid = (bias - b_hi.astype(F32)).astype(BF16)
    b_lo = (bias - b_hi.astype(F32) - b_mid.astype(F32)).astype(BF16)
    terms = jnp.pad(jnp.stack([b_hi, b_mid, b_lo]), ((0, 13), (0, feat - hidden)))
    pack = jnp.concatenate([weight.T, cotangent.T, terms], axis=0)
    dense = call(
        functools.partial(dense_kernel, zl_n),
        shape(x_n, c_n, zl_n, tile, tile),
        sources,
        tiles,
        smem=1,
    )

    quarters = to_all(features.reshape(y_n, rows, feat), "y")
    mine = lax.dynamic_index_in_dim(quarters, my_x, 0, keepdims=False)
    def along_x(v, step):
        return lax.ppermute(v, "x", [(x, (x + step) % x_n) for x in range(x_n)])

    mine, dense = lax.optimization_barrier((mine, dense))
    shares = [along_x(dense[step], step) for step in range(1, x_n)]
    column = to_all(jnp.broadcast_to(mine[None], (zl_n, rows, feat)), "zl")
    column = lax.all_gather(column, "c")
    if x_n > 2:
        column, shares[1] = lax.optimization_barrier((column, shares[1]))
    pieces = ([dense[0]] + shares + [dense[0]] * 2)[:4]
    blocks = to_all(jnp.broadcast_to(column[None], (y_n,) + column.shape), "y")

    a_mine, part = call(
        forward_kernel,
        (shape(c_n, zl_n, tile, tile), shape(x_n, tile + pack.shape[0], feat)),
        *pieces,
        blocks,
        pack,
    )
    summed = call(
        functools.partial(row_sum_kernel, hidden),
        shape(tile + x_n * 2 * hidden + 16, feat),
        to_all(part, "x"),
    )
    summed_other = swap(summed, "zh")

    payload = shape(y_n, zl_n * rows + EXTRA, tile)
    act_t, keep, give = call(
        functools.partial(backward_kernel, x_n),
        (shape(hidden, tile), payload, payload),
        summed,
        summed_other,
        pack,
        a_mine,
    )
    both = (keep.astype(F32) + swap(give, "c").astype(F32)).astype(BF16)
    across = to_all(both, "y")
    up = call(plane_sum_kernel, shape(zl_n, zh_n, rows + EXTRA, feat), across).reshape(
        zl_n * zh_n, rows + EXTRA, feat
    )
    down = to_all(up, ("zl", "zh"))
    last = call(
        functools.partial(column_sum_kernel, zl_n, zh_n), shape(y_n * x_n, rows + EXTRA, feat), down
    )
    feature_grad, wgrad_t, bias_grad = call(
        functools.partial(finish_kernel, y_n, x_n),
        (shape(tile, feat, dtype=F32), shape(hidden, feat, dtype=F32), shape(1, hidden, dtype=F32)),
        to_all(last, ("y", "x")),
    )
    return act_t.T, feature_grad, wgrad_t.T, bias_grad[0]


def split_mesh(mesh, sizes):
    return Mesh(mesh.devices.reshape(tuple(sizes[a] for a in AXES)), AXES)


def solution(mesh, sizes=None):
    sizes = sizes or {"y": 4, "zl": 8, "c": 2, "x": 4, "zh": 2}
    placed = (
        P(BLK, None),
        P(BLK, HID, None, None, None),
        P(BLK, HID, None),
        P(None, HID),
        P(HID),
        P(BLK, HID),
    )
    return jax.shard_map(
        functools.partial(on_device, sizes),
        mesh=split_mesh(mesh, sizes),
        in_specs=placed,
        out_specs=(P(BLK, HID), P(BLK, None), P(None, HID), P(HID)),
        check_vma=False,
    )
```

```python
import functools

import jax
import jax.numpy as jnp
from jax import lax
from jax.experimental import pallas as pl
from jax.experimental.pallas import tpu as pltpu
from jax.sharding import Mesh
from jax.sharding import PartitionSpec as P

BF16 = jnp.bfloat16
F32 = jnp.float32
AXES = ("y", "zl", "c", "x", "zh")
BLK = ("y", "zl", "c")
HID = ("x", "zh")
EXTRA = 16
SCALE = 0.7978845608028654
CUBIC = 0.044715
PARAMS = pltpu.CompilerParams(vmem_limit_bytes=48 * 1024 * 1024)


def mm(a, b, ca, cb):
    return lax.dot_general(a, b, (((ca,), (cb,)), ((), ())), preferred_element_type=F32)


def slope(v):
    t = jnp.tanh(SCALE * (v + CUBIC * (v * v * v)))
    du = SCALE * (1.0 + (3.0 * CUBIC) * (v * v))
    return 0.5 * (1.0 + t) + 0.5 * v * (1.0 - t * t) * du


def dense_kernel(zl_n, src_ref, tiles_ref, out_ref):
    my_c, my_x = lax.axis_index("c"), lax.axis_index("x")
    x_n = out_ref.shape[0]
    out_ref[...] = jnp.zeros_like(out_ref)
    acc = None
    for k in range(tiles_ref.shape[0]):
        src = src_ref[k]
        piece = tiles_ref[k].astype(F32)
        if k:
            piece = piece + jnp.where(src == src_ref[k - 1], acc, 0.0)
        acc = piece
        y, zl, c = src // (2 * zl_n), (src // 2) % zl_n, src % 2
        at = (pl.ds((y + x_n - my_x) % x_n, 1), pl.ds(jnp.where(c == my_c, 0, 1), 1), pl.ds(zl, 1))
        out_ref[at] = acc.astype(BF16)[None, None, None]


def forward_kernel(d0_ref, d1_ref, d2_ref, d3_ref, feat_ref, pack_ref, pack_other_ref, a_ref, out_ref):
    my_c = lax.axis_index("c")
    tile = d0_ref.shape[-1]
    feat = feat_ref.shape[-1]
    size = pack_ref.shape[0]
    zl_n = d0_ref.shape[1]
    acc = jnp.zeros((tile, feat), F32)
    for core in range(2):
        for zl in range(zl_n):
            total = d0_ref[core, zl].astype(F32)
            for ref in (d1_ref, d2_ref, d3_ref)[: out_ref.shape[0] - 1]:
                total = total + ref[core, zl].astype(F32)
            total = total.astype(BF16)
            a_ref[core, zl] = total
            at = (slice(None), pl.ds(my_c if core == 0 else 1 - my_c, 1), slice(zl, zl + 1))
            acc = acc + mm(total, feat_ref[at].reshape(tile, feat), 1, 0)
    part = acc.astype(BF16)
    for x in range(out_ref.shape[0]):
        out_ref[x, :tile, :] = part
        out_ref[x, tile : tile + size, :] = pack_ref[...]
        out_ref[x, tile + size :, :] = pack_other_ref[...]


def backward_kernel(sum_ref, other_ref, packs_ref, pack_ref, a_ref, act_ref, out_ref):
    my_c = lax.axis_index("c")
    x_n = packs_ref.shape[0]
    hidden = act_ref.shape[0]
    tile = a_ref.shape[-1]
    zl_n = a_ref.shape[1]
    size = pack_ref.shape[0]
    y_n = out_ref.shape[0]
    rows = tile // y_n
    agg = (sum_ref[...].astype(F32) + other_ref[...].astype(F32)).astype(BF16)
    starts = [(x, tile + z * size) for x in range(x_n) for z in range(2)]

    def gather(start, count):
        return jnp.concatenate([packs_ref[x, at + start : at + start + count, :] for x, at in starts], axis=0)

    def bias_of(three):
        return mm(three, jnp.ones((three.shape[0], tile), BF16), 0, 0)[:hidden]

    w_t = gather(0, hidden)
    cot_t = gather(hidden, hidden)
    bias_t = jnp.concatenate([bias_of(packs_ref[x, at + 2 * hidden : at + size, :]) for x, at in starts], axis=0)
    pre_t = mm(w_t, agg, 1, 1) + bias_t
    grad_t = (cot_t.astype(F32) * slope(pre_t)).astype(BF16)
    back_t = mm(w_t, grad_t, 0, 0).astype(BF16)

    w_mine = pack_ref[0:hidden, :]
    mine_t = mm(w_mine, agg, 1, 1) + bias_of(pack_ref[2 * hidden :, :])
    t = jnp.tanh(SCALE * (mine_t + CUBIC * (mine_t * mine_t * mine_t)))
    act_ref[...] = (mine_t * (0.5 * (1.0 + t))).astype(BF16)
    grad_mine = (pack_ref[hidden : 2 * hidden, :].astype(F32) * slope(mine_t)).astype(BF16)
    wgrad = mm(grad_mine, agg, 1, 0)
    bgrad = mm(jnp.ones((8, tile), BF16), grad_mine, 1, 1)
    bgrad = jnp.concatenate([bgrad, jnp.zeros((8, tile - hidden), F32)], axis=1)

    body = zl_n * rows
    share = hidden // y_n
    assert share <= 8
    for y in range(y_n):
        piece = [wgrad[y * share : (y + 1) * share], bgrad]
        if share < 8:
            piece.insert(1, jnp.zeros((8 - share, tile), F32))
        piece = jnp.concatenate(piece, axis=0).astype(BF16)
        out_ref[y, 0, body:, :] = piece
        out_ref[y, 1, body:, :] = piece
    for core in range(2):
        to = pl.ds(my_c if core == 0 else 1 - my_c, 1)
        for zl in range(0, zl_n, 2):
            pair = mm(back_t, jnp.concatenate([a_ref[core, zl], a_ref[core, zl + 1]], axis=1), 1, 0).astype(BF16)
            for y in range(y_n):
                part = pair[y * rows : (y + 1) * rows]
                out_ref[y, to, zl * rows : (zl + 1) * rows, :] = part[None, :, :tile]
                out_ref[y, to, (zl + 1) * rows : (zl + 2) * rows, :] = part[None, :, tile:]


def plane_sum_kernel(in_ref, out_ref):
    zl_n, zh_n, size, _ = out_ref.shape
    rows = size - EXTRA
    total = in_ref[0].astype(F32)
    for y in range(1, in_ref.shape[0]):
        total = total + in_ref[y].astype(F32)
    total = total.astype(BF16)
    for z in range(zl_n):
        for h in range(zh_n):
            out_ref[z, h, :rows, :] = total[z * rows : (z + 1) * rows]
            out_ref[z, h, rows:, :] = total[zl_n * rows :]


def column_sum_kernel(zl_n, zh_n, in_ref, out_ref):
    my_zh = lax.axis_index("zh")
    rows = in_ref.shape[1] - EXTRA
    total = in_ref[0, :rows, :].astype(F32)
    for s in range(1, zl_n * zh_n):
        total = total + in_ref[s, :rows, :].astype(F32)
    extra = in_ref[my_zh, rows:, :].astype(F32)
    for z in range(1, zl_n):
        extra = extra + in_ref[z * zh_n + my_zh, rows:, :].astype(F32)
    for s in range(out_ref.shape[0]):
        out_ref[s, :rows, :] = total.astype(out_ref.dtype)
        out_ref[s, rows:, :] = extra.astype(out_ref.dtype)


def finish_kernel(y_n, x_n, in_ref, feat_ref, wgrad_ref, bgrad_ref):
    my_x, my_y = lax.axis_index("x"), lax.axis_index("y")
    rows = in_ref.shape[1] - EXTRA
    hidden = bgrad_ref.shape[1]
    share = hidden // y_n
    feat_ref[...] = jnp.concatenate(
        [in_ref[y * x_n + my_y, :rows, :].astype(F32) for y in range(y_n)], axis=0
    ).T
    pieces = [in_ref[y * x_n + my_x, rows:, :].astype(F32) for y in range(y_n)]
    wgrad_ref[...] = jnp.concatenate([p[:share] for p in pieces], axis=0)
    bgrad_ref[...] = pieces[0][8:9, :hidden]


VMEM = pl.BlockSpec(memory_space=pltpu.VMEM)
SMEM = pl.BlockSpec(memory_space=pltpu.SMEM)


def shape(*dims, dtype=BF16):
    return jax.ShapeDtypeStruct(dims, dtype)


def call(kernel, out, *args, smem=0):
    many = isinstance(out, (tuple, list))
    return pl.pallas_call(
        kernel,
        out_shape=out,
        in_specs=[SMEM] * smem + [VMEM] * (len(args) - smem),
        out_specs=[VMEM] * len(out) if many else VMEM,
        compiler_params=PARAMS,
    )(*args)


def to_all(v, axes):
    return lax.all_to_all(v, axes, 0, 0, tiled=True)


def swap(v, axis):
    return lax.ppermute(v, axis, [(0, 1), (1, 0)])


def on_device(sizes, features, tile_values, tile_block, weight, bias, cotangent):
    y_n, zl_n, c_n, x_n, zh_n = (sizes[a] for a in AXES)
    tile = tile_values.shape[-1]
    feat = features.shape[1]
    hidden = bias.shape[0]
    rows = tile // y_n
    tiles = tile_values.reshape(-1, tile, tile)
    sources = tile_block.reshape(-1)
    my_x = lax.axis_index("x")

    b_hi = bias.astype(BF16)
    b_mid = (bias - b_hi.astype(F32)).astype(BF16)
    b_lo = (bias - b_hi.astype(F32) - b_mid.astype(F32)).astype(BF16)
    terms = jnp.pad(jnp.stack([b_hi, b_mid, b_lo]), ((0, 13), (0, feat - hidden)))
    pack = jnp.concatenate([weight.T, cotangent.T, terms], axis=0)
    dense = call(
        functools.partial(dense_kernel, zl_n),
        shape(x_n, c_n, zl_n, tile, tile),
        sources,
        tiles,
        smem=1,
    )

    quarters = to_all(features.reshape(y_n, rows, feat), "y")
    mine = lax.dynamic_index_in_dim(quarters, my_x, 0, keepdims=False)
    mine, dense = lax.optimization_barrier((mine, dense))
    pieces = [dense[0]]
    for step in range(1, x_n):
        pieces.append(lax.ppermute(dense[step], "x", [(x, (x + step) % x_n) for x in range(x_n)]))
    while len(pieces) < 4:
        pieces.append(pieces[0])
    column = to_all(jnp.broadcast_to(mine[None], (zl_n, rows, feat)), "zl")
    column, pack = lax.optimization_barrier((column, pack))
    pack_other = swap(pack, "zh")
    blocks = to_all(jnp.broadcast_to(column[None], (y_n * c_n,) + column.shape), ("y", "c"))
    blocks = blocks.reshape((y_n, c_n) + column.shape)

    size = pack.shape[0]
    a_mine, part = call(
        forward_kernel,
        (shape(c_n, zl_n, tile, tile), shape(x_n, tile + 2 * size, feat)),
        *pieces,
        blocks,
        pack,
        pack_other,
    )
    part = to_all(part, "x")
    summed = jnp.sum(part[:, :tile].astype(F32), axis=0).astype(BF16)
    summed_other = swap(summed, "zh")

    act_t, sent = call(
        backward_kernel,
        (shape(hidden, tile), shape(y_n, c_n, zl_n * rows + EXTRA, tile)),
        summed,
        summed_other,
        part,
        pack,
        a_mine,
    )
    across = to_all(sent.reshape(y_n * c_n, zl_n * rows + EXTRA, tile), ("y", "c"))
    up = call(plane_sum_kernel, shape(zl_n, zh_n, rows + EXTRA, feat), across).reshape(
        zl_n * zh_n, rows + EXTRA, feat
    )
    down = to_all(up, ("zl", "zh"))
    last = call(
        functools.partial(column_sum_kernel, zl_n, zh_n), shape(y_n * x_n, rows + EXTRA, feat), down
    )
    feature_grad, wgrad_t, bias_grad = call(
        functools.partial(finish_kernel, y_n, x_n),
        (shape(tile, feat, dtype=F32), shape(hidden, feat, dtype=F32), shape(1, hidden, dtype=F32)),
        to_all(last, ("y", "x")),
    )
    return act_t.T, feature_grad, wgrad_t.T, bias_grad[0]


def split_mesh(mesh, sizes):
    return Mesh(mesh.devices.reshape(tuple(sizes[a] for a in AXES)), AXES)


def solution(mesh, sizes=None):
    sizes = sizes or {"y": 4, "zl": 8, "c": 2, "x": 4, "zh": 2}
    placed = (
        P(BLK, None),
        P(BLK, HID, None, None, None),
        P(BLK, HID, None),
        P(None, HID),
        P(HID),
        P(BLK, HID),
    )
    return jax.shard_map(
        functools.partial(on_device, sizes),
        mesh=split_mesh(mesh, sizes),
        in_specs=placed,
        out_specs=(P(BLK, HID), P(BLK, None), P(None, HID), P(HID)),
        check_vma=False,
    )
```

```python
import functools

import jax
import jax.numpy as jnp
from jax import lax
from jax.experimental import pallas as pl
from jax.experimental.pallas import tpu as pltpu
from jax.sharding import Mesh
from jax.sharding import PartitionSpec as P

BF16 = jnp.bfloat16
F32 = jnp.float32
AXES = ("y", "zl", "c", "x", "zh")
BLK = ("y", "zl", "c")
HID = ("x", "zh")
EXTRA = 16
SCALE = 0.7978845608028654
CUBIC = 0.044715
PARAMS = pltpu.CompilerParams(vmem_limit_bytes=48 * 1024 * 1024)


def mm(a, b, ca, cb):
    return lax.dot_general(a, b, (((ca,), (cb,)), ((), ())), preferred_element_type=F32)


def slope(v):
    t = jnp.tanh(SCALE * (v + CUBIC * (v * v * v)))
    du = SCALE * (1.0 + (3.0 * CUBIC) * (v * v))
    return 0.5 * (1.0 + t) + 0.5 * v * (1.0 - t * t) * du


def dense_kernel(zl_n, src_ref, tiles_ref, out_ref):
    my_c, my_x = lax.axis_index("c"), lax.axis_index("x")
    out_ref[...] = jnp.zeros_like(out_ref)
    acc = None
    for k in range(tiles_ref.shape[0]):
        src = src_ref[k]
        piece = tiles_ref[k].astype(F32)
        if k:
            piece = piece + jnp.where(src == src_ref[k - 1], acc, 0.0)
        acc = piece
        y, zl, c = src // (2 * zl_n), (src // 2) % zl_n, src % 2
        apart = y ^ my_x
        slot = jnp.where(apart == 0, 0, jnp.where(apart == 3, 1, apart + 1))
        at = (pl.ds(slot, 1), pl.ds(jnp.where(c == my_c, 0, 1), 1), pl.ds(zl, 1))
        out_ref[at] = acc.astype(BF16)[None, None, None]


def relay_kernel(mine_ref, other_ref, out_ref):
    out_ref[...] = (mine_ref[1].astype(F32) + other_ref[1].astype(F32)).astype(BF16)


def forward_kernel(d0_ref, d1_ref, d2_ref, feat_ref, pack_ref, pack_other_ref, a_ref, out_ref):
    my_c = lax.axis_index("c")
    tile = a_ref.shape[-1]
    feat = feat_ref.shape[-1]
    size = pack_ref.shape[0]
    zl_n = a_ref.shape[1]
    acc = jnp.zeros((tile, feat), F32)
    for core in range(2):
        for zl in range(zl_n):
            total = d0_ref[0, core, zl].astype(F32) + d1_ref[0, core, zl].astype(F32)
            total = (total + d2_ref[core, zl].astype(F32)).astype(BF16)
            a_ref[core, zl] = total
            at = (slice(None), pl.ds(my_c if core == 0 else 1 - my_c, 1), slice(zl, zl + 1))
            acc = acc + mm(total, feat_ref[at].reshape(tile, feat), 1, 0)
    part = acc.astype(BF16)
    for x in range(out_ref.shape[0]):
        out_ref[x, :tile, :] = part
        out_ref[x, tile : tile + size, :] = pack_ref[...]
        out_ref[x, tile + size :, :] = pack_other_ref[...]


def backward_kernel(sum_ref, other_ref, packs_ref, pack_ref, a_ref, act_ref, out_ref):
    my_c = lax.axis_index("c")
    x_n = packs_ref.shape[0]
    hidden = act_ref.shape[0]
    tile = a_ref.shape[-1]
    zl_n = a_ref.shape[1]
    size = pack_ref.shape[0]
    y_n = out_ref.shape[0]
    rows = tile // y_n
    agg = (sum_ref[...].astype(F32) + other_ref[...].astype(F32)).astype(BF16)
    starts = [(x, tile + z * size) for x in range(x_n) for z in range(2)]

    def gather(start, count):
        return jnp.concatenate([packs_ref[x, at + start : at + start + count, :] for x, at in starts], axis=0)

    def bias_of(three):
        return mm(three, jnp.ones((three.shape[0], tile), BF16), 0, 0)[:hidden]

    w_t = gather(0, hidden)
    cot_t = gather(hidden, hidden)
    bias_t = jnp.concatenate([bias_of(packs_ref[x, at + 2 * hidden : at + size, :]) for x, at in starts], axis=0)
    pre_t = mm(w_t, agg, 1, 1) + bias_t
    grad_t = (cot_t.astype(F32) * slope(pre_t)).astype(BF16)
    back_t = mm(w_t, grad_t, 0, 0).astype(BF16)

    w_mine = pack_ref[0:hidden, :]
    mine_t = mm(w_mine, agg, 1, 1) + bias_of(pack_ref[2 * hidden :, :])
    t = jnp.tanh(SCALE * (mine_t + CUBIC * (mine_t * mine_t * mine_t)))
    act_ref[...] = (mine_t * (0.5 * (1.0 + t))).astype(BF16)
    grad_mine = (pack_ref[hidden : 2 * hidden, :].astype(F32) * slope(mine_t)).astype(BF16)
    wgrad = mm(grad_mine, agg, 1, 0)
    bgrad = mm(jnp.ones((8, tile), BF16), grad_mine, 1, 1)
    bgrad = jnp.concatenate([bgrad, jnp.zeros((8, tile - hidden), F32)], axis=1)

    body = zl_n * rows
    share = hidden // y_n
    assert share <= 8
    for y in range(y_n):
        piece = [wgrad[y * share : (y + 1) * share], bgrad]
        if share < 8:
            piece.insert(1, jnp.zeros((8 - share, tile), F32))
        piece = jnp.concatenate(piece, axis=0).astype(BF16)
        out_ref[y, 0, body:, :] = piece
        out_ref[y, 1, body:, :] = piece
    for core in range(2):
        to = pl.ds(my_c if core == 0 else 1 - my_c, 1)
        for zl in range(0, zl_n, 2):
            pair = mm(back_t, jnp.concatenate([a_ref[core, zl], a_ref[core, zl + 1]], axis=1), 1, 0).astype(BF16)
            for y in range(y_n):
                part = pair[y * rows : (y + 1) * rows]
                out_ref[y, to, zl * rows : (zl + 1) * rows, :] = part[None, :, :tile]
                out_ref[y, to, (zl + 1) * rows : (zl + 2) * rows, :] = part[None, :, tile:]


def plane_sum_kernel(in_ref, out_ref):
    zl_n, zh_n, size, _ = out_ref.shape
    rows = size - EXTRA
    total = in_ref[0].astype(F32)
    for y in range(1, in_ref.shape[0]):
        total = total + in_ref[y].astype(F32)
    total = total.astype(BF16)
    for z in range(zl_n):
        for h in range(zh_n):
            out_ref[z, h, :rows, :] = total[z * rows : (z + 1) * rows]
            out_ref[z, h, rows:, :] = total[zl_n * rows :]


def column_sum_kernel(zl_n, zh_n, in_ref, out_ref):
    my_zh = lax.axis_index("zh")
    rows = in_ref.shape[1] - EXTRA
    total = in_ref[0, :rows, :].astype(F32)
    for s in range(1, zl_n * zh_n):
        total = total + in_ref[s, :rows, :].astype(F32)
    extra = in_ref[my_zh, rows:, :].astype(F32)
    for z in range(1, zl_n):
        extra = extra + in_ref[z * zh_n + my_zh, rows:, :].astype(F32)
    for s in range(out_ref.shape[0]):
        out_ref[s, :rows, :] = total.astype(out_ref.dtype)
        out_ref[s, rows:, :] = extra.astype(out_ref.dtype)


def finish_kernel(y_n, x_n, in_ref, feat_ref, wgrad_ref, bgrad_ref):
    my_x, my_y = lax.axis_index("x"), lax.axis_index("y")
    rows = in_ref.shape[1] - EXTRA
    hidden = bgrad_ref.shape[1]
    share = hidden // y_n
    feat_ref[...] = jnp.concatenate(
        [in_ref[y * x_n + my_y, :rows, :].astype(F32) for y in range(y_n)], axis=0
    ).T
    pieces = [in_ref[y * x_n + my_x, rows:, :].astype(F32) for y in range(y_n)]
    wgrad_ref[...] = jnp.concatenate([p[:share] for p in pieces], axis=0)
    bgrad_ref[...] = pieces[0][8:9, :hidden]


VMEM = pl.BlockSpec(memory_space=pltpu.VMEM)
SMEM = pl.BlockSpec(memory_space=pltpu.SMEM)


def shape(*dims, dtype=BF16):
    return jax.ShapeDtypeStruct(dims, dtype)


def call(kernel, out, *args, smem=0):
    many = isinstance(out, (tuple, list))
    return pl.pallas_call(
        kernel,
        out_shape=out,
        in_specs=[SMEM] * smem + [VMEM] * (len(args) - smem),
        out_specs=[VMEM] * len(out) if many else VMEM,
        compiler_params=PARAMS,
    )(*args)


def to_all(v, axes):
    return lax.all_to_all(v, axes, 0, 0, tiled=True)


def swap(v, axis):
    return lax.ppermute(v, axis, [(0, 1), (1, 0)])


def on_device(sizes, features, tile_values, tile_block, weight, bias, cotangent):
    y_n, zl_n, c_n, x_n, zh_n = (sizes[a] for a in AXES)
    tile = tile_values.shape[-1]
    feat = features.shape[1]
    hidden = bias.shape[0]
    rows = tile // y_n
    tiles = tile_values.reshape(-1, tile, tile)
    sources = tile_block.reshape(-1)
    my_x = lax.axis_index("x")

    b_hi = bias.astype(BF16)
    b_mid = (bias - b_hi.astype(F32)).astype(BF16)
    b_lo = (bias - b_hi.astype(F32) - b_mid.astype(F32)).astype(BF16)
    terms = jnp.pad(jnp.stack([b_hi, b_mid, b_lo]), ((0, 13), (0, feat - hidden)))
    pack = jnp.concatenate([weight.T, cotangent.T, terms], axis=0)
    dense = call(
        functools.partial(dense_kernel, zl_n),
        shape(x_n, c_n, zl_n, tile, tile),
        sources,
        tiles,
        smem=1,
    )

    quarters = to_all(features.reshape(y_n, rows, feat), "y")
    mine = lax.dynamic_index_in_dim(quarters, my_x, 0, keepdims=False)
    mine, dense, pack = lax.optimization_barrier((mine, dense, pack))
    near = lax.ppermute(dense[2:], "x", [(x, x ^ 1) for x in range(x_n)])
    pack_other = swap(pack, "zh")
    column = to_all(jnp.broadcast_to(mine[None], (zl_n, rows, feat)), "zl")
    near, pack_other = lax.optimization_barrier((near, pack_other))
    relay = call(relay_kernel, shape(c_n, zl_n, tile, tile), dense[:2], near)
    far = lax.ppermute(relay, "x", [(x, x_n - 1 - x) for x in range(x_n)])
    column, relay = lax.optimization_barrier((column, relay))
    blocks = to_all(jnp.broadcast_to(column[None], (y_n * c_n,) + column.shape), ("y", "c"))
    blocks = blocks.reshape((y_n, c_n) + column.shape)

    size = pack.shape[0]
    a_mine, part = call(
        forward_kernel,
        (shape(c_n, zl_n, tile, tile), shape(x_n, tile + 2 * size, feat)),
        dense[:2],
        near,
        far,
        blocks,
        pack,
        pack_other,
    )
    part = to_all(part, "x")
    summed = jnp.sum(part[:, :tile].astype(F32), axis=0).astype(BF16)
    summed_other = swap(summed, "zh")

    act_t, sent = call(
        backward_kernel,
        (shape(hidden, tile), shape(y_n, c_n, zl_n * rows + EXTRA, tile)),
        summed,
        summed_other,
        part,
        pack,
        a_mine,
    )
    across = to_all(sent.reshape(y_n * c_n, zl_n * rows + EXTRA, tile), ("y", "c"))
    up = call(plane_sum_kernel, shape(zl_n, zh_n, rows + EXTRA, feat), across).reshape(
        zl_n * zh_n, rows + EXTRA, feat
    )
    down = to_all(up, ("zl", "zh"))
    last = call(
        functools.partial(column_sum_kernel, zl_n, zh_n), shape(y_n * x_n, rows + EXTRA, feat), down
    )
    feature_grad, wgrad_t, bias_grad = call(
        functools.partial(finish_kernel, y_n, x_n),
        (shape(tile, feat, dtype=F32), shape(hidden, feat, dtype=F32), shape(1, hidden, dtype=F32)),
        to_all(last, ("y", "x")),
    )
    return act_t.T, feature_grad, wgrad_t.T, bias_grad[0]


def split_mesh(mesh, sizes):
    return Mesh(mesh.devices.reshape(tuple(sizes[a] for a in AXES)), AXES)


def solution(mesh, sizes=None):
    sizes = sizes or {"y": 4, "zl": 8, "c": 2, "x": 4, "zh": 2}
    placed = (
        P(BLK, None),
        P(BLK, HID, None, None, None),
        P(BLK, HID, None),
        P(None, HID),
        P(HID),
        P(BLK, HID),
    )
    return jax.shard_map(
        functools.partial(on_device, sizes),
        mesh=split_mesh(mesh, sizes),
        in_specs=placed,
        out_specs=(P(BLK, HID), P(BLK, None), P(None, HID), P(HID)),
        check_vma=False,
    )
```

```python
import functools

import jax
import jax.numpy as jnp
from jax import lax
from jax.experimental import pallas as pl
from jax.experimental.pallas import tpu as pltpu
from jax.sharding import Mesh
from jax.sharding import PartitionSpec as P

BF16 = jnp.bfloat16
F32 = jnp.float32
AXES = ("y", "zl", "c", "x", "zh")
BLK = ("y", "zl", "c")
HID = ("x", "zh")
EXTRA = 16
SCALE = 0.7978845608028654
CUBIC = 0.044715
PARAMS = pltpu.CompilerParams(vmem_limit_bytes=48 * 1024 * 1024)


def mm(a, b, ca, cb):
    return lax.dot_general(a, b, (((ca,), (cb,)), ((), ())), preferred_element_type=F32)


def slope(v):
    t = jnp.tanh(SCALE * (v + CUBIC * (v * v * v)))
    du = SCALE * (1.0 + (3.0 * CUBIC) * (v * v))
    return 0.5 * (1.0 + t) + 0.5 * v * (1.0 - t * t) * du


def dense_kernel(zl_n, src_ref, tiles_ref, bias_ref, out_ref, terms_ref):
    bias = bias_ref[...]
    high = bias.astype(BF16).astype(F32)
    middle = (bias - high).astype(BF16).astype(F32)
    rows = jnp.concatenate([high, middle, bias - high - middle, jnp.zeros((13, bias.shape[1]), F32)], axis=0)
    fill = jnp.zeros((16, terms_ref.shape[1] - bias.shape[1]), F32)
    terms_ref[...] = jnp.concatenate([rows, fill], axis=1).astype(BF16)
    my_c, my_x = lax.axis_index("c"), lax.axis_index("x")
    x_n = out_ref.shape[0]
    out_ref[...] = jnp.zeros_like(out_ref)
    acc = None
    for k in range(tiles_ref.shape[0]):
        src = src_ref[k]
        piece = tiles_ref[k].astype(F32)
        if k:
            piece = piece + jnp.where(src == src_ref[k - 1], acc, 0.0)
        acc = piece
        y, zl, c = src // (2 * zl_n), (src // 2) % zl_n, src % 2
        at = (pl.ds((y + x_n - my_x) % x_n, 1), pl.ds(jnp.where(c == my_c, 0, 1), 1), pl.ds(zl, 1))
        out_ref[at] = acc.astype(BF16)[None, None, None]


def forward_kernel(d0_ref, d1_ref, d2_ref, d3_ref, feat_ref, pack_ref, pack_other_ref, a_ref, out_ref):
    my_c = lax.axis_index("c")
    tile = d0_ref.shape[-1]
    feat = feat_ref.shape[-1]
    size = pack_ref.shape[0]
    zl_n = d0_ref.shape[1]
    acc = jnp.zeros((tile, feat), F32)
    for core in range(2):
        for zl in range(zl_n):
            total = d0_ref[core, zl].astype(F32)
            for ref in (d1_ref, d2_ref, d3_ref)[: out_ref.shape[0] - 1]:
                total = total + ref[core, zl].astype(F32)
            total = total.astype(BF16)
            a_ref[core, zl] = total
            at = (slice(None), pl.ds(my_c if core == 0 else 1 - my_c, 1), slice(zl, zl + 1))
            acc = acc + mm(total, feat_ref[at].reshape(tile, feat), 1, 0)
    part = acc.astype(BF16)
    for x in range(out_ref.shape[0]):
        out_ref[x, :tile, :] = part
        out_ref[x, tile : tile + size, :] = pack_ref[...]
        out_ref[x, tile + size :, :] = pack_other_ref[...]


def backward_kernel(sum_ref, other_ref, packs_ref, pack_ref, a_ref, act_ref, out_ref):
    my_c = lax.axis_index("c")
    x_n = packs_ref.shape[0]
    hidden = act_ref.shape[0]
    tile = a_ref.shape[-1]
    zl_n = a_ref.shape[1]
    size = pack_ref.shape[0]
    y_n = out_ref.shape[0]
    rows = tile // y_n
    agg = (sum_ref[...].astype(F32) + other_ref[...].astype(F32)).astype(BF16)
    starts = [(x, tile + z * size) for x in range(x_n) for z in range(2)]

    def gather(start, count):
        return jnp.concatenate([packs_ref[x, at + start : at + start + count, :] for x, at in starts], axis=0)

    def bias_of(three):
        return mm(three, jnp.ones((three.shape[0], tile), BF16), 0, 0)[:hidden]

    w_t = gather(0, hidden)
    cot_t = gather(hidden, hidden)
    bias_t = jnp.concatenate([bias_of(packs_ref[x, at + 2 * hidden : at + size, :]) for x, at in starts], axis=0)
    pre_t = mm(w_t, agg, 1, 1) + bias_t
    grad_t = (cot_t.astype(F32) * slope(pre_t)).astype(BF16)
    back_t = mm(w_t, grad_t, 0, 0).astype(BF16)

    w_mine = pack_ref[0:hidden, :]
    mine_t = mm(w_mine, agg, 1, 1) + bias_of(pack_ref[2 * hidden :, :])
    t = jnp.tanh(SCALE * (mine_t + CUBIC * (mine_t * mine_t * mine_t)))
    act_ref[...] = (mine_t * (0.5 * (1.0 + t))).astype(BF16)
    grad_mine = (pack_ref[hidden : 2 * hidden, :].astype(F32) * slope(mine_t)).astype(BF16)
    wgrad = mm(grad_mine, agg, 1, 0)
    bgrad = mm(jnp.ones((8, tile), BF16), grad_mine, 1, 1)
    bgrad = jnp.concatenate([bgrad, jnp.zeros((8, tile - hidden), F32)], axis=1)

    body = zl_n * rows
    share = hidden // y_n
    assert share <= 8
    for y in range(y_n):
        piece = [wgrad[y * share : (y + 1) * share], bgrad]
        if share < 8:
            piece.insert(1, jnp.zeros((8 - share, tile), F32))
        piece = jnp.concatenate(piece, axis=0).astype(BF16)
        out_ref[y, 0, body:, :] = piece
        out_ref[y, 1, body:, :] = piece
    for core in range(2):
        to = pl.ds(my_c if core == 0 else 1 - my_c, 1)
        for zl in range(0, zl_n, 2):
            pair = mm(back_t, jnp.concatenate([a_ref[core, zl], a_ref[core, zl + 1]], axis=1), 1, 0).astype(BF16)
            for y in range(y_n):
                part = pair[y * rows : (y + 1) * rows]
                out_ref[y, to, zl * rows : (zl + 1) * rows, :] = part[None, :, :tile]
                out_ref[y, to, (zl + 1) * rows : (zl + 2) * rows, :] = part[None, :, tile:]


def plane_sum_kernel(in_ref, out_ref):
    zl_n, zh_n, size, _ = out_ref.shape
    rows = size - EXTRA
    total = in_ref[0].astype(F32)
    for y in range(1, in_ref.shape[0]):
        total = total + in_ref[y].astype(F32)
    total = total.astype(BF16)
    for z in range(zl_n):
        for h in range(zh_n):
            out_ref[z, h, :rows, :] = total[z * rows : (z + 1) * rows]
            out_ref[z, h, rows:, :] = total[zl_n * rows :]


def column_sum_kernel(zl_n, zh_n, in_ref, out_ref):
    my_zh = lax.axis_index("zh")
    rows = in_ref.shape[1] - EXTRA
    total = in_ref[0, :rows, :].astype(F32)
    for s in range(1, zl_n * zh_n):
        total = total + in_ref[s, :rows, :].astype(F32)
    extra = in_ref[my_zh, rows:, :].astype(F32)
    for z in range(1, zl_n):
        extra = extra + in_ref[z * zh_n + my_zh, rows:, :].astype(F32)
    for s in range(out_ref.shape[0]):
        out_ref[s, :rows, :] = total.astype(out_ref.dtype)
        out_ref[s, rows:, :] = extra.astype(out_ref.dtype)


def finish_kernel(y_n, x_n, in_ref, feat_ref, wgrad_ref, bgrad_ref):
    my_x, my_y = lax.axis_index("x"), lax.axis_index("y")
    rows = in_ref.shape[1] - EXTRA
    hidden = bgrad_ref.shape[1]
    share = hidden // y_n
    feat_ref[...] = jnp.concatenate(
        [in_ref[y * x_n + my_y, :rows, :].astype(F32) for y in range(y_n)], axis=0
    ).T
    pieces = [in_ref[y * x_n + my_x, rows:, :].astype(F32) for y in range(y_n)]
    wgrad_ref[...] = jnp.concatenate([p[:share] for p in pieces], axis=0)
    bgrad_ref[...] = pieces[0][8:9, :hidden]


VMEM = pl.BlockSpec(memory_space=pltpu.VMEM)
SMEM = pl.BlockSpec(memory_space=pltpu.SMEM)


def shape(*dims, dtype=BF16):
    return jax.ShapeDtypeStruct(dims, dtype)


def call(kernel, out, *args, smem=0):
    many = isinstance(out, (tuple, list))
    return pl.pallas_call(
        kernel,
        out_shape=out,
        in_specs=[SMEM] * smem + [VMEM] * (len(args) - smem),
        out_specs=[VMEM] * len(out) if many else VMEM,
        compiler_params=PARAMS,
    )(*args)


def to_all(v, axes):
    return lax.all_to_all(v, axes, 0, 0, tiled=True)


def swap(v, axis):
    return lax.ppermute(v, axis, [(0, 1), (1, 0)])


def on_device(sizes, features, tile_values, tile_block, weight, bias, cotangent):
    y_n, zl_n, c_n, x_n, zh_n = (sizes[a] for a in AXES)
    tile = tile_values.shape[-1]
    feat = features.shape[1]
    hidden = bias.shape[0]
    rows = tile // y_n
    tiles = tile_values.reshape(-1, tile, tile)
    sources = tile_block.reshape(-1)
    my_x = lax.axis_index("x")

    dense, terms = call(
        functools.partial(dense_kernel, zl_n),
        (shape(x_n, c_n, zl_n, tile, tile), shape(16, feat)),
        sources,
        tiles,
        bias[None],
        smem=1,
    )
    pack = jnp.concatenate([weight.T, cotangent.T, terms], axis=0)

    quarters = to_all(features.reshape(y_n, rows, feat), "y")
    mine = lax.dynamic_index_in_dim(quarters, my_x, 0, keepdims=False)
    mine, dense = lax.optimization_barrier((mine, dense))
    pieces = [dense[0]]
    for step in range(1, x_n):
        pieces.append(lax.ppermute(dense[step], "x", [(x, (x + step) % x_n) for x in range(x_n)]))
    while len(pieces) < 4:
        pieces.append(pieces[0])
    column = to_all(jnp.broadcast_to(mine[None], (zl_n, rows, feat)), "zl")
    column, pack = lax.optimization_barrier((column, pack))
    pack_other = swap(pack, "zh")
    blocks = to_all(jnp.broadcast_to(column[None], (y_n * c_n,) + column.shape), ("y", "c"))
    blocks = blocks.reshape((y_n, c_n) + column.shape)

    size = pack.shape[0]
    a_mine, part = call(
        forward_kernel,
        (shape(c_n, zl_n, tile, tile), shape(x_n, tile + 2 * size, feat)),
        *pieces,
        blocks,
        pack,
        pack_other,
    )
    part = to_all(part, "x")
    summed = jnp.sum(part[:, :tile].astype(F32), axis=0).astype(BF16)
    summed_other = swap(summed, "zh")

    act_t, sent = call(
        backward_kernel,
        (shape(hidden, tile), shape(y_n, c_n, zl_n * rows + EXTRA, tile)),
        summed,
        summed_other,
        part,
        pack,
        a_mine,
    )
    across = to_all(sent.reshape(y_n * c_n, zl_n * rows + EXTRA, tile), ("y", "c"))
    up = call(plane_sum_kernel, shape(zl_n, zh_n, rows + EXTRA, feat), across).reshape(
        zl_n * zh_n, rows + EXTRA, feat
    )
    down = to_all(up, ("zl", "zh"))
    last = call(
        functools.partial(column_sum_kernel, zl_n, zh_n), shape(y_n * x_n, rows + EXTRA, feat), down
    )
    feature_grad, wgrad_t, bias_grad = call(
        functools.partial(finish_kernel, y_n, x_n),
        (shape(tile, feat, dtype=F32), shape(hidden, feat, dtype=F32), shape(1, hidden, dtype=F32)),
        to_all(last, ("y", "x")),
    )
    return act_t.T, feature_grad, wgrad_t.T, bias_grad[0]


def split_mesh(mesh, sizes):
    return Mesh(mesh.devices.reshape(tuple(sizes[a] for a in AXES)), AXES)


def solution(mesh, sizes=None):
    sizes = sizes or {"y": 4, "zl": 8, "c": 2, "x": 4, "zh": 2}
    placed = (
        P(BLK, None),
        P(BLK, HID, None, None, None),
        P(BLK, HID, None),
        P(None, HID),
        P(HID),
        P(BLK, HID),
    )
    return jax.shard_map(
        functools.partial(on_device, sizes),
        mesh=split_mesh(mesh, sizes),
        in_specs=placed,
        out_specs=(P(BLK, HID), P(BLK, None), P(None, HID), P(HID)),
        check_vma=False,
    )
```
